128 devices in a mesh: seq: 16 (over z, x), head: 8 (over y, core).
Axes of the slice: x: 4, y: 4, z: 4, core: 2. Of those that a mesh axis runs over, the one named last changes fastest.
Arguments:
- hidden: bfloat16 [2, 4, 8192], P(None, None, 'seq'), may hold values from -6 to 6
- w_query: bfloat16 [8192, 8192], P('seq', 'head'), may hold values from -0.0625 to 0.0625
- key_matrix: bfloat16 [8192, 1024], P('seq', 'head'), may hold values from -0.25 to 0.25
- value_matrix: bfloat16 [8192, 1024], P('seq', 'head'), may hold values from -0.0625 to 0.0625
- w_out: bfloat16 [8192, 8192], P('head', 'seq'), may hold values from -0.0625 to 0.0625
- key_cache: bfloat16 [4, 131072, 1024], P(None, 'seq', 'head'), may hold values from -250 to 250, as said below
- stored_value_cache: bfloat16 [4, 131072, 1024], P(None, 'seq', 'head'), may hold values from -6 to 6
- lengths: int32 [4], replicated, may hold values from 8192 to 131072, as said below
Outputs:
- attn_out: bfloat16 [2, 4, 8192], P(None, None, ('seq', 'head'))
- new_keys: bfloat16 [2, 4, 1024], P(None, None, 'head')
- new_values: bfloat16 [2, 4, 1024], P(None, None, 'head')
The draws below stay inside these ranges and needn't reach their ends.
Inputs may be any that keep to these rules, and one draw needn't show every extreme that they name: `key_cache`: cached keys, already rotated to their positions. `lengths`: in every draw one sequence fills all 131072 cached positions.
All inputs are finite; a program needn't handle non-finite values.
Results may differ from the reference program's by a relative error of at most 0.02.
Values may be sent and summed in bfloat16 or wider, within the bound.
No kernel may reach another device: no remote copies, remote signals or barrier semaphores. Data moves between devices by JAX's collectives and lax.ppermute only.
A program may use at most 64 MiB of HBM per device.

```python
import jax
import jax.numpy as jnp
import numpy as np
from jax import lax

MODEL_WIDTH = 8192
QUERY_HEADS = 64
KEY_HEADS = 8
HEAD_WIDTH = 128
BATCH_ROWS = 4
STEPS = 2
BLOCK_POSITIONS = 512
CONTEXT_LENGTH = 131072
N_HEAD = 8


def draw_key_cache(key, part):
    key = jax.random.fold_in(key, 11)
    base_key = jax.random.fold_in(key, 0)
    target_shape = (BATCH_ROWS, CONTEXT_LENGTH, KEY_HEADS * HEAD_WIDTH)
    key_rows = 2.0 * jax.random.truncated_normal(base_key, -4.0, 4.0, target_shape, jnp.float32)
    return key_rows.astype(jnp.bfloat16)


def draw_lengths(key, part):
    key = jax.random.fold_in(key, 23)
    value_key, pick_key = jax.random.split(key)
    drawn = jax.random.randint(value_key, (BATCH_ROWS,), CONTEXT_LENGTH // 16, CONTEXT_LENGTH + 1)
    chosen = jax.random.randint(pick_key, (), 0, BATCH_ROWS)
    return jnp.where(jnp.arange(BATCH_ROWS) == chosen, CONTEXT_LENGTH, drawn).astype(jnp.int32)


def block_levels(own_key, shape, cuts, least, high):
    loudness = 1.0
    for dim, shards_of in cuts:
        steps = jax.random.uniform(jax.random.fold_in(jax.random.fold_in(own_key, 6), dim), (shards_of,), jnp.float32, least / len(cuts), high / len(cuts))
        loudness = loudness * jnp.repeat(jnp.exp(steps), shape[dim] // shards_of).reshape((-1,) + (1,) * (len(shape) - 1 - dim))
    return loudness


def bell_draw(stream_key, dims, deviation, limit, cuts=(), kind=jnp.bfloat16):
    values = deviation * jax.random.normal(stream_key, dims, jnp.float32)
    if cuts:
        values = values * block_levels(stream_key, dims, cuts, -0.22, 0.18)
    return jnp.clip(values, -limit, limit).astype(kind)


def setup_inputs(seed: int = 0) -> dict:
    key_list = jax.random.split(jax.random.key(seed), 9)
    return {
        "hidden": bell_draw(key_list[0], (STEPS, BATCH_ROWS, MODEL_WIDTH), 1.0, 6.0, ((2, 16),)),
        "w_query": bell_draw(key_list[1], (MODEL_WIDTH, QUERY_HEADS * HEAD_WIDTH), MODEL_WIDTH ** -0.5, 0.0625, ((0, 16), (1, 8))),
        "key_matrix": bell_draw(key_list[2], (MODEL_WIDTH, KEY_HEADS * HEAD_WIDTH), (MODEL_WIDTH // 16) ** -0.5, 0.25, ((0, 16), (1, 8))),
        "value_matrix": bell_draw(key_list[3], (MODEL_WIDTH, KEY_HEADS * HEAD_WIDTH), MODEL_WIDTH ** -0.5, 0.0625, ((0, 16), (1, 8))),
        "w_out": bell_draw(key_list[4], (QUERY_HEADS * HEAD_WIDTH, MODEL_WIDTH), (QUERY_HEADS * HEAD_WIDTH) ** -0.5, 0.0625, ((0, 8), (1, 16))),
        "key_cache": draw_key_cache(jax.random.fold_in(key_list[8], 71), 0),
        "stored_value_cache": bell_draw(key_list[6], (BATCH_ROWS, CONTEXT_LENGTH, KEY_HEADS * HEAD_WIDTH), 1.0, 6.0, ((1, 16), (2, 8))),
        "lengths": draw_lengths(jax.random.fold_in(key_list[8], 71), 0),
    }


theta_base = 500000.0
negative_fill = -1.0e30


def apply_rotary(input_vectors, token_positions):
    half_dim = input_vectors.shape[-1] // 2
    exponent = np.arange(half_dim) * 2.0 / input_vectors.shape[-1]
    inverse = theta_base ** (-exponent)
    coarse = np.mod(1024.0 * inverse, 2.0 * np.pi)
    fine_table = jnp.asarray(inverse, jnp.float32)
    coarse_table = jnp.asarray(coarse, jnp.float32)
    upper_part = (token_positions // 1024).astype(jnp.float32)[..., None]
    lower_part = (token_positions % 1024).astype(jnp.float32)[..., None]
    angles = upper_part * coarse_table + lower_part * fine_table
    cosine = jnp.cos(angles)
    sine_part = jnp.sin(angles)
    first_half = input_vectors[..., :half_dim]
    second_half = input_vectors[..., half_dim:]
    return jnp.concatenate([first_half * cosine - second_half * sine_part, second_half * cosine + first_half * sine_part], axis=-1)


def attend(query_rows, key_rows, value_rows, length, newest_keys, newest_values):
    queries_per_group = QUERY_HEADS // KEY_HEADS
    softmax_blocks = CONTEXT_LENGTH // BLOCK_POSITIONS
    broadcast_query = query_rows.reshape(KEY_HEADS, queries_per_group, HEAD_WIDTH).astype(jnp.float32)
    broadcast_keys = key_rows.reshape(softmax_blocks, BLOCK_POSITIONS, KEY_HEADS, HEAD_WIDTH).astype(jnp.float32)
    broadcast_values = value_rows.reshape(softmax_blocks, BLOCK_POSITIONS, KEY_HEADS, HEAD_WIDTH).astype(jnp.float32)
    scores = jnp.einsum('kgd,ntkd->kgnt', broadcast_query, broadcast_keys)
    valid = (jnp.arange(CONTEXT_LENGTH, dtype=jnp.int32) < length).reshape(softmax_blocks, BLOCK_POSITIONS)
    block_top = jnp.max(jnp.where(valid, scores, negative_fill), axis=-1)
    weights = jnp.where(valid, jnp.exp(scores - block_top[..., None]), 0.0)
    weights = lax.optimization_barrier(weights.astype(jnp.bfloat16)).astype(jnp.float32)
    block_sum = jnp.sum(weights, axis=-1)
    block_out = jnp.einsum('kgnt,ntkd->kgnd', weights, broadcast_values)
    newest_count = newest_keys.shape[0]
    newest_key = newest_keys.reshape(newest_count, KEY_HEADS, HEAD_WIDTH).astype(jnp.float32)
    newest_value = newest_values.reshape(newest_count, KEY_HEADS, HEAD_WIDTH).astype(jnp.float32)
    fresh_scores = jnp.einsum('kgd,tkd->kgt', broadcast_query, newest_key)
    fresh_top = jnp.max(fresh_scores, axis=-1)
    fresh_weights = jnp.exp(fresh_scores - fresh_top[..., None])
    fresh_weights = lax.optimization_barrier(fresh_weights.astype(jnp.bfloat16)).astype(jnp.float32)
    fresh_sum = jnp.sum(fresh_weights, axis=-1)
    fresh_out = jnp.einsum('kgt,tkd->kgd', fresh_weights, newest_value)
    overall = jnp.maximum(jnp.max(block_top, axis=-1), fresh_top)
    factors = jnp.exp(block_top - overall[..., None])
    fresh_factor = jnp.exp(fresh_top - overall)
    totals = jnp.sum(factors * block_sum, axis=-1) + fresh_factor * fresh_sum
    mixed = jnp.sum(factors[..., None] * block_out, axis=2) + fresh_factor[..., None] * fresh_out
    return (mixed / totals[..., None]).reshape(QUERY_HEADS * HEAD_WIDTH).astype(jnp.bfloat16)


def reference(hidden, w_query, key_matrix, value_matrix, w_out, key_cache, stored_value_cache, lengths):
    score_scale = HEAD_WIDTH ** -0.5
    keys_list = []
    values_list = []
    raw_values = []
    head_rows = []
    for step_index in range(STEPS):
        step_inputs = hidden[step_index]
        query_raw = jnp.dot(step_inputs, w_query, preferred_element_type=jnp.float32).reshape(BATCH_ROWS, QUERY_HEADS, HEAD_WIDTH)
        unrotated_key = jnp.dot(step_inputs, key_matrix, preferred_element_type=jnp.float32).reshape(BATCH_ROWS, KEY_HEADS, HEAD_WIDTH)
        value_raw = jnp.dot(step_inputs, value_matrix, preferred_element_type=jnp.float32)
        token_positions = (lengths + step_index).astype(jnp.int32)[:, None]
        query_rows = (apply_rotary(query_raw, token_positions) * score_scale).astype(jnp.bfloat16)
        appended_key = apply_rotary(unrotated_key, token_positions).astype(jnp.bfloat16).reshape(BATCH_ROWS, KEY_HEADS * HEAD_WIDTH)
        keys_list.append(appended_key)
        values_list.append(value_raw.astype(jnp.bfloat16))
        raw_values.append(value_raw)
        newest_keys = jnp.stack(keys_list, axis=1)
        newest_values = jnp.stack(raw_values, axis=1)
        outputs = []
        for batch_index in range(BATCH_ROWS):
            outputs.append(attend(query_rows[batch_index], key_cache[batch_index], stored_value_cache[batch_index], lengths[batch_index], newest_keys[batch_index], newest_values[batch_index]))
        head_rows.append(jnp.stack(outputs))
    heads = jnp.stack(head_rows).reshape(STEPS * BATCH_ROWS, QUERY_HEADS * HEAD_WIDTH)
    group_width = QUERY_HEADS * HEAD_WIDTH // N_HEAD
    total = jnp.zeros((STEPS * BATCH_ROWS, MODEL_WIDTH), jnp.float32)
    for group_index in range(N_HEAD):
        part_rows = heads[:, group_index * group_width:(group_index + 1) * group_width]
        part_weights = w_out[group_index * group_width:(group_index + 1) * group_width]
        partial_out = jnp.dot(part_rows, part_weights, preferred_element_type=jnp.float32).astype(jnp.bfloat16)
        total = total + partial_out.astype(jnp.float32)
    attn_out = total.astype(jnp.bfloat16).reshape(STEPS, BATCH_ROWS, MODEL_WIDTH)
    return attn_out, jnp.stack(keys_list), jnp.stack(values_list)
```

```python
import functools

import jax
import jax.numpy as jnp
import numpy as np
from jax import lax
from jax.experimental import pallas as pl
from jax.experimental.pallas import tpu as pltpu
from jax.sharding import PartitionSpec as P

HEAD_WIDTH = 128
HALF = HEAD_WIDTH // 2
THETA = 500000.0
FILL = -1e30
F32 = jnp.float32
BF16 = jnp.bfloat16
VMEM = pltpu.MemorySpace.VMEM
SMEM = pltpu.MemorySpace.SMEM


def rotary_tables():
    exponent = np.arange(HALF) * 2.0 / HEAD_WIDTH
    inverse = THETA ** (-exponent)
    coarse = np.mod(1024.0 * inverse, 2.0 * np.pi)
    fine = np.concatenate([inverse, inverse])[None]
    coarse = np.concatenate([coarse, coarse])[None]
    return np.concatenate([fine, coarse]).astype(np.float32)


def project_kernel(copies, hidden_ref, wq_ref, wk_ref, wv_ref, out_ref):
    steps, batch, _ = hidden_ref.shape
    rows = jnp.concatenate([hidden_ref[s].astype(F32) for s in range(steps)], axis=0).astype(BF16)
    q_width = wq_ref.shape[1]
    kv_width = wk_ref.shape[1]
    query = jnp.dot(rows, wq_ref[...], preferred_element_type=F32).astype(BF16)
    key = jnp.dot(rows, wk_ref[...], preferred_element_type=F32).astype(BF16)
    value = jnp.dot(rows, wv_ref[...], preferred_element_type=F32).astype(BF16)
    for c in range(copies):
        out_ref[c, :, :q_width] = query
        out_ref[c, :, q_width : q_width + kv_width] = key
        out_ref[c, :, q_width + kv_width :] = value


def attend_kernel(
    steps, heads, chunk, copies, seq_ref, lengths_ref, sums_ref, cos_ref, sin_ref, keys_ref, values_ref,
    message_ref, new_keys_ref, new_values_ref, query_scr, scores_scr, out_scr,
):
    batch, context, width = keys_ref.shape
    rows = steps * batch
    group = steps * heads
    total = sums_ref[0].astype(F32)
    for d in range(1, sums_ref.shape[0]):
        total = total + sums_ref[d].astype(F32)
    cosine = cos_ref[...]
    sine = sin_ref[...]

    def rotate(x):
        return x * cosine + pltpu.roll(x, HALF, 1) * sine

    for h in range(heads):
        rotated = rotate(total[:, h * width : (h + 1) * width]) * (width**-0.5)
        for r in range(rows):
            s, b = divmod(r, batch)
            query_scr[b, s * heads + h : s * heads + h + 1, :] = rotated[r : r + 1]
    new_key = rotate(total[:, heads * width : (heads + 1) * width]).astype(BF16)
    new_value = total[:, (heads + 1) * width :]
    for s in range(steps):
        new_keys_ref[s] = new_key.astype(F32)[s * batch : (s + 1) * batch].astype(BF16)
        new_values_ref[s] = new_value[s * batch : (s + 1) * batch].astype(BF16)
    new_key = new_key.astype(F32)

    seq = seq_ref[0]
    owner = seq == 0
    sublane = lax.broadcasted_iota(jnp.int32, (group, width), 0)
    lane = lax.broadcasted_iota(jnp.int32, (group, width), 1)
    head_of = sublane % heads
    stat_lane = lane - head_of
    position = lax.broadcasted_iota(jnp.int32, (group, chunk), 1)
    row_step = lax.broadcasted_iota(jnp.int32, (group, 1), 0) // heads

    for b in range(batch):
        query = query_scr[b].astype(BF16)
        limit = lengths_ref[b] - seq * context
        top = jnp.full((group, chunk), FILL, F32)
        for start in range(0, context, chunk):
            scores = lax.dot_general(
                query, keys_ref[b, start : start + chunk, :], (((1,), (1,)), ((), ())),
                preferred_element_type=F32,
            )
            scores = jnp.where(position < limit - start, scores, FILL)
            scores_scr[:, start : start + chunk] = scores
            top = jnp.maximum(top, scores)
        top = jnp.max(top, axis=1, keepdims=True)
        query_wide = query.astype(F32)
        fresh = []
        for t in range(steps):
            row = t * batch + b
            score = jnp.sum(query_wide * new_key[row : row + 1], axis=1, keepdims=True)
            fresh.append(jnp.where(row_step >= t, score, FILL))
        fresh_top = functools.reduce(jnp.maximum, fresh)
        top = jnp.where(owner, jnp.maximum(top, fresh_top), top)
        top = top.astype(BF16).astype(F32)
        weight_sum = jnp.zeros((group, chunk), F32)
        out = jnp.zeros((group, width), F32)
        for start in range(0, context, chunk):
            weights = jnp.where(
                position < limit - start, jnp.exp(scores_scr[:, start : start + chunk] - top), 0.0
            ).astype(BF16)
            weight_sum = weight_sum + weights.astype(F32)
            out = out + jnp.dot(
                weights, values_ref[b, start : start + chunk, :], preferred_element_type=F32
            )
        weight_sum = jnp.sum(weight_sum, axis=1, keepdims=True)
        fresh_scale = jnp.where(owner, jnp.exp(fresh_top - jnp.where(owner, top, fresh_top)), 0.0)
        for t in range(steps):
            row = t * batch + b
            weight = jnp.where(row_step >= t, jnp.exp(fresh[t] - fresh_top), 0.0)
            weight = weight.astype(BF16).astype(F32) * fresh_scale
            weight_sum = weight_sum + weight
            out = out + weight * new_value[row : row + 1]
        sum_high = weight_sum.astype(BF16).astype(F32)
        sum_low = weight_sum - sum_high
        stats = jnp.where(
            stat_lane == 0, top,
            jnp.where(stat_lane == heads, sum_high, jnp.where(stat_lane == 2 * heads, sum_low, 0.0)),
        )
        for s in range(steps):
            r = s * batch + b
            out_scr[r : r + 1, heads * width :] = jnp.sum(
                stats[s * heads : (s + 1) * heads], axis=0, keepdims=True
            )
            for h in range(heads):
                out_scr[r : r + 1, h * width : (h + 1) * width] = out[s * heads + h : s * heads + h + 1]
    message = out_scr[...].astype(BF16)
    for c in range(copies):
        message_ref[c] = message


def combine_kernel(heads, head_ref, message_ref, w_out_ref, out_ref):
    devices, rows, _ = message_ref.shape
    width = HEAD_WIDTH
    stats = [message_ref[d, :, heads * width :].astype(F32) for d in range(devices)]
    top = functools.reduce(jnp.maximum, stats)
    total = jnp.zeros((rows, width), F32)
    factors = []
    lane = lax.broadcasted_iota(jnp.int32, (rows, width), 1)
    for d in range(devices):
        factor = jnp.exp(jnp.where(lane < heads, stats[d] - top, 0.0))
        sums = pltpu.roll(stats[d], width - heads, 1) + pltpu.roll(stats[d], width - 2 * heads, 1)
        total = total + factor * sums
        factors.append(factor)
    scale = 1.0 / jnp.where(lane < heads, total, 1.0)
    factors = [f * scale for f in factors]
    attended = []
    for h in range(heads):
        mixed = jnp.zeros((rows, width), F32)
        for d in range(devices):
            part = message_ref[d, :, h * width : (h + 1) * width].astype(F32)
            mixed = mixed + factors[d][:, h : h + 1] * part
        attended.append(mixed.astype(BF16))
    attended = jnp.concatenate(attended, axis=1)
    projected = jnp.dot(attended, w_out_ref[...], preferred_element_type=F32).astype(BF16)
    rank = head_ref[0] // 2
    ranks = out_ref.shape[0]
    for target in range(ranks):
        slot = lax.rem(target - rank + ranks, ranks)
        out_ref[slot] = projected[:, target * width : (target + 1) * width]


def in_vmem(x):
    return pltpu.with_memory_space_constraint(x, VMEM)


def gather_all(x, axis):
    return lax.all_to_all(x, axis, 0, 0, tiled=True)


def local(hidden, w_query, key_matrix, value_matrix, w_out, key_cache, value_cache, lengths):
    steps, batch, _ = hidden.shape
    rows = steps * batch
    width = HEAD_WIDTH
    heads = w_query.shape[1] // width
    devices = lax.axis_size("seq")
    seq = lax.axis_index("seq").astype(jnp.int32).reshape(1)
    head = lax.axis_index("head").astype(jnp.int32)
    whole = pl.BlockSpec(memory_space=VMEM)
    scalar = pl.BlockSpec(memory_space=SMEM)

    positions = (lengths[None, :] + jnp.arange(steps, dtype=jnp.int32)[:, None]).reshape(rows, 1)
    tables = jnp.asarray(rotary_tables())
    angles = (positions // 1024).astype(F32) * tables[1:2] + (positions % 1024).astype(F32) * tables[0:1]
    sign = jnp.asarray(np.where(np.arange(width) < HALF, -1.0, 1.0).astype(np.float32))[None]
    cosine = jnp.cos(angles)
    sine = jnp.sin(angles) * sign

    with jax.named_scope("projections"):
        partial_sums = pl.pallas_call(
            functools.partial(project_kernel, devices),
            out_shape=jax.ShapeDtypeStruct((devices, rows, (heads + 2) * width), BF16),
            in_specs=[whole] * 4,
            out_specs=whole,
        )(hidden, w_query, key_matrix, value_matrix)
    with jax.named_scope("sum_over_width"):
        sums = gather_all(partial_sums, "seq")
    with jax.named_scope("attention"):
        message, new_keys, new_values = pl.pallas_call(
            functools.partial(attend_kernel, steps, heads, 2048, devices),
            out_shape=(
                jax.ShapeDtypeStruct((devices, rows, (heads + 1) * width), BF16),
                jax.ShapeDtypeStruct((steps, batch, width), BF16),
                jax.ShapeDtypeStruct((steps, batch, width), BF16),
            ),
            in_specs=[scalar, scalar] + [whole] * 5,
            out_specs=(whole, whole, whole),
            scratch_shapes=[
                pltpu.VMEM((batch, steps * heads, width), F32),
                pltpu.VMEM((steps * heads, key_cache.shape[1]), F32),
                pltpu.VMEM((rows, (heads + 1) * width), F32),
            ],
            compiler_params=pltpu.CompilerParams(vmem_limit_bytes=8 * 2**20),
        )(seq, lengths, sums, cosine, sine, in_vmem(key_cache), in_vmem(value_cache))
    with jax.named_scope("combine"):
        messages = gather_all(message, "seq")
        ranks = lax.axis_size("head") // 2
        projected = pl.pallas_call(
            functools.partial(combine_kernel, heads),
            out_shape=jax.ShapeDtypeStruct((ranks, rows, width), BF16),
            in_specs=[scalar, whole, whole],
            out_specs=whole,
        )(head.reshape(1), in_vmem(messages), in_vmem(w_out))
    with jax.named_scope("sum_over_heads"):
        parts = [projected[0]]
        for d in range(1, ranks):
            route = [(2 * y + c, 2 * ((y + d) % ranks) + c) for y in range(ranks) for c in range(2)]
            parts.append(lax.ppermute(projected[d], "head", route))
        pair = sum(p.astype(F32) for p in parts)
        core = head % 2
        mine = jnp.where(core == 0, pair[:, :HALF], pair[:, HALF:])
        other = jnp.where(core == 0, pair[:, HALF:], pair[:, :HALF])
        other = lax.ppermute(other, "head", [(i, i ^ 1) for i in range(2 * ranks)])
        attn_out = (mine + other).astype(BF16).reshape(steps, batch, HALF)
    return attn_out, new_keys, new_values


def solution(mesh):
    in_specs = (
        P(None, None, "seq"),
        P("seq", "head"),
        P("seq", "head"),
        P("seq", "head"),
        P("head", "seq"),
        P(None, "seq", "head"),
        P(None, "seq", "head"),
        P(),
    )
    out_specs = (P(None, None, ("seq", "head")), P(None, None, "head"), P(None, None, "head"))
    return jax.shard_map(local, mesh=mesh, in_specs=in_specs, out_specs=out_specs, check_vma=False)
```

```python
import functools

import jax
import jax.numpy as jnp
import numpy as np
from jax import lax
from jax.experimental import pallas as pl
from jax.experimental.pallas import tpu as pltpu
from jax.sharding import PartitionSpec as P

HEAD_WIDTH = 128
HALF = HEAD_WIDTH // 2
THETA = 500000.0
FILL = -1e30
F32 = jnp.float32
BF16 = jnp.bfloat16
VMEM = pltpu.MemorySpace.VMEM


def rotary_tables():
    exponent = np.arange(HALF) * 2.0 / HEAD_WIDTH
    inverse = THETA ** (-exponent)
    coarse = np.mod(1024.0 * inverse, 2.0 * np.pi)
    fine = np.concatenate([inverse, inverse])[None]
    coarse = np.concatenate([coarse, coarse])[None]
    sign = np.where(np.arange(HEAD_WIDTH) < HALF, -1.0, 1.0)[None]
    return np.concatenate([fine, coarse, sign]).astype(np.float32)


def note_kernel(x_ref, o_ref):
    o_ref[...] = x_ref[...]


def project_kernel(
    steps, constants_hbm, lengths_hbm, hidden_hbm, wk_hbm, wv_hbm, wq_hbm, _, __, out_ref, tables_ref,
    constants_ref, lengths_ref, hidden_ref, wk_ref, wv_ref, wq_ref, sems,
):
    pairs = [
        (constants_hbm, constants_ref), (lengths_hbm, lengths_ref), (hidden_hbm, hidden_ref),
        (wk_hbm, wk_ref), (wv_hbm, wv_ref), (wq_hbm, wq_ref),
    ]
    copies = [pltpu.make_async_copy(src, dst, sems.at[i]) for i, (src, dst) in enumerate(pairs)]
    for copy in copies:
        copy.start()
    copies[0].wait()
    copies[1].wait()
    batch = lengths_ref.shape[0]
    rows = steps * batch
    width = constants_ref.shape[1]
    sublane = lax.broadcasted_iota(jnp.int32, (rows, width), 0)
    position = jnp.zeros((rows, width), jnp.int32)
    for r in range(rows):
        s, b = divmod(r, batch)
        position = jnp.where(sublane == r, lengths_ref[b] + s, position)
    upper = jnp.right_shift(position, 10).astype(F32)
    lower = jnp.bitwise_and(position, 1023).astype(F32)
    angles = upper * constants_ref[1:2, :] + lower * constants_ref[0:1, :]
    tables_ref[:rows, :] = jnp.cos(angles)
    tables_ref[rows : 2 * rows, :] = jnp.sin(angles) * constants_ref[2:3, :]
    tables_ref[2 * rows :, :] = position.astype(F32)
    copies[2].wait()
    hidden = jnp.concatenate([hidden_ref[s].astype(F32) for s in range(steps)], axis=0).astype(BF16)
    q_width = wq_ref.shape[1]
    kv_width = wk_ref.shape[1]
    copies[3].wait()
    key = jnp.dot(hidden, wk_ref[...], preferred_element_type=F32)
    out_ref[:, q_width : q_width + kv_width] = key.astype(BF16)
    copies[4].wait()
    value = jnp.dot(hidden, wv_ref[...], preferred_element_type=F32)
    out_ref[:, q_width + kv_width :] = value.astype(BF16)
    copies[5].wait()
    query = jnp.dot(hidden, wq_ref[...], preferred_element_type=F32)
    out_ref[:, :q_width] = query.astype(BF16)


def fetch_kernel(first, source_ref, target_ref, sem):
    batch = target_ref.shape[0]
    copies = [
        pltpu.make_async_copy(source_ref.at[first + b], target_ref.at[b], sem.at[b]) for b in range(batch)
    ]
    for copy in copies:
        copy.start()
    for copy in copies:
        copy.wait()


def attend_kernel(
    steps, heads, chunk, copies, tables_ref, sum0_ref, sum1_ref, sum2_ref, sum3_ref, *refs
):
    *keys_refs, values_ref, message_ref, new_keys_hbm, new_values_hbm = refs[:-8]
    query_scr, scores_scr, out_scr, value_buf, new_keys_ref, new_values_ref, value_sems, new_sems = refs[-8:]
    batch, context, width = values_ref.shape
    each = batch // len(keys_refs)

    def fetch(b):
        return pltpu.make_async_copy(values_ref.at[b], value_buf.at[b], value_sems.at[b])

    rows = steps * batch
    group = steps * heads
    total = sum0_ref[...].astype(F32)
    for part_ref in (sum1_ref, sum2_ref, sum3_ref):
        total = total + part_ref[...].astype(F32)
    cosine = tables_ref[:rows]
    sine = tables_ref[rows : 2 * rows]

    def rotate(x):
        return x * cosine + pltpu.roll(x, HALF, 1) * sine

    for h in range(heads):
        rotated = rotate(total[:, h * width : (h + 1) * width]) * (width**-0.5)
        for r in range(rows):
            s, b = divmod(r, batch)
            query_scr[b, s * heads + h : s * heads + h + 1, :] = rotated[r : r + 1]
    new_key = rotate(total[:, heads * width : (heads + 1) * width]).astype(BF16).astype(F32)
    new_value = total[:, (heads + 1) * width :]
    for s in range(steps):
        new_keys_ref[s] = new_key[s * batch : (s + 1) * batch].astype(BF16)
        new_values_ref[s] = new_value[s * batch : (s + 1) * batch].astype(BF16)
    new_copies = [
        pltpu.make_async_copy(new_keys_ref, new_keys_hbm, new_sems.at[0]),
        pltpu.make_async_copy(new_values_ref, new_values_hbm, new_sems.at[1]),
    ]
    for copy in new_copies:
        copy.start()

    seq = lax.axis_index("seq")
    first = seq * context
    owner = seq == 0
    sublane = lax.broadcasted_iota(jnp.int32, (group, width), 0)
    lane = lax.broadcasted_iota(jnp.int32, (group, width), 1)
    stat_lane = lane - sublane % heads
    position = lax.broadcasted_iota(jnp.int32, (group, chunk), 1)
    row_step = lax.broadcasted_iota(jnp.int32, (group, 1), 0) // heads

    tops = []
    for b in range(batch):
        query = query_scr[b].astype(BF16)
        keys_ref = keys_refs[b // each]
        limit = tables_ref[2 * rows + b : 2 * rows + b + 1, :1].astype(jnp.int32) - first
        top = jnp.full((group, chunk), FILL, F32)
        for start in range(0, context, chunk):
            scores = lax.dot_general(
                query, keys_ref[b % each, start : start + chunk, :], (((1,), (1,)), ((), ())),
                preferred_element_type=F32,
            )
            scores = jnp.where(position < limit - start, scores, FILL)
            scores_scr[b, :, start : start + chunk] = scores
            top = jnp.maximum(top, scores)
        tops.append(jnp.max(top, axis=1, keepdims=True))
    for b in range(batch):
        limit = tables_ref[2 * rows + b : 2 * rows + b + 1, :1].astype(jnp.int32) - first
        top = tops[b]
        query_wide = query_scr[b].astype(BF16).astype(F32)
        fresh = []
        for t in range(steps):
            row = t * batch + b
            score = jnp.sum(query_wide * new_key[row : row + 1], axis=1, keepdims=True)
            fresh.append(jnp.where(row_step >= t, score, FILL))
        fresh_top = functools.reduce(jnp.maximum, fresh)
        top = jnp.where(owner, jnp.maximum(top, fresh_top), top)
        top = top.astype(BF16).astype(F32)
        weight_sum = jnp.zeros((group, chunk), F32)
        out = jnp.zeros((group, width), F32)
        for start in range(0, context, chunk):
            weights = jnp.where(
                position < limit - start, jnp.exp(scores_scr[b, :, start : start + chunk] - top), 0.0
            ).astype(BF16)
            weight_sum = weight_sum + weights.astype(F32)
            out = out + jnp.dot(
                weights, values_ref[b, start : start + chunk, :], preferred_element_type=F32
            )
        weight_sum = jnp.sum(weight_sum, axis=1, keepdims=True)
        fresh_scale = jnp.where(owner, jnp.exp(fresh_top - jnp.where(owner, top, fresh_top)), 0.0)
        for t in range(steps):
            row = t * batch + b
            weight = jnp.where(row_step >= t, jnp.exp(fresh[t] - fresh_top), 0.0)
            weight = weight.astype(BF16).astype(F32) * fresh_scale
            weight_sum = weight_sum + weight
            out = out + weight * new_value[row : row + 1]
        sum_high = weight_sum.astype(BF16).astype(F32)
        sum_low = weight_sum - sum_high
        stats = jnp.where(
            stat_lane == 0, top,
            jnp.where(stat_lane == heads, sum_high, jnp.where(stat_lane == 2 * heads, sum_low, 0.0)),
        )
        for s in range(steps):
            r = s * batch + b
            out_scr[r : r + 1, heads * width :] = jnp.sum(
                stats[s * heads : (s + 1) * heads], axis=0, keepdims=True
            )
            for h in range(heads):
                out_scr[r : r + 1, h * width : (h + 1) * width] = out[s * heads + h : s * heads + h + 1]
    message = out_scr[...].astype(BF16)
    for c in range(copies):
        message_ref[c] = message
    for copy in new_copies:
        copy.wait()


def combine_kernel(heads, message_ref, w_out_ref, mine_ref, other_ref):
    devices, rows, _ = message_ref.shape
    width = HEAD_WIDTH
    stats = [message_ref[d, :, heads * width :].astype(F32) for d in range(devices)]
    top = functools.reduce(jnp.maximum, stats)
    total = jnp.zeros((rows, width), F32)
    factors = []
    lane = lax.broadcasted_iota(jnp.int32, (rows, width), 1)
    for d in range(devices):
        factor = jnp.exp(jnp.where(lane < heads, stats[d] - top, 0.0))
        sums = pltpu.roll(stats[d], width - heads, 1) + pltpu.roll(stats[d], width - 2 * heads, 1)
        total = total + factor * sums
        factors.append(factor)
    scale = 1.0 / jnp.where(lane < heads, total, 1.0)
    factors = [f * scale for f in factors]
    attended = []
    for h in range(heads):
        mixed = jnp.zeros((rows, width), F32)
        for d in range(devices):
            part = message_ref[d, :, h * width : (h + 1) * width].astype(F32)
            mixed = mixed + factors[d][:, h : h + 1] * part
        attended.append(mixed.astype(BF16))
    attended = jnp.concatenate(attended, axis=1)
    projected = jnp.dot(attended, w_out_ref[...], preferred_element_type=F32)
    head = lax.axis_index("head")
    rank = head // 2
    first_core = head % 2 == 0
    for target in range(mine_ref.shape[0]):
        block = projected[:, target * width : (target + 1) * width]
        swapped = pltpu.roll(block, HALF, 1)
        slot = jnp.bitwise_xor(rank, target)
        mine_ref[slot] = jnp.where(first_core, block, swapped)[:, :HALF].astype(BF16)
        other_ref[slot] = jnp.where(first_core, swapped, block)[:, :HALF].astype(BF16)


def in_vmem(x):
    return pltpu.with_memory_space_constraint(x, VMEM)


def exchange_routes(count, inner, axis_inner, order=(1, 3, 2)):
    routes = []
    for d in order:
        pairs = []
        for i in range(count):
            for j in range(inner):
                pairs.append((i * inner + j, (i ^ d) * inner + j) if axis_inner else (j * count + i, j * count + (i ^ d)))
        routes.append(pairs)
    return routes


def in_hbm(x):
    return pltpu.with_memory_space_constraint(x, pltpu.MemorySpace.HBM)


def gather_all(x, axis):
    return lax.all_to_all(x, axis, 0, 0, tiled=True)


def local(hidden, w_query, key_matrix, value_matrix, w_out, key_cache, value_cache, lengths):
    steps, batch, _ = hidden.shape
    rows = steps * batch
    width = HEAD_WIDTH
    heads = w_query.shape[1] // width
    devices = lax.axis_size("seq")
    whole = pl.BlockSpec(memory_space=VMEM)
    anywhere = pl.BlockSpec(memory_space=pl.ANY)

    with jax.named_scope("projections"):
        operands = (jnp.asarray(rotary_tables()), lengths, hidden, key_matrix, value_matrix, w_query)
        buffers = [
            (pltpu.SMEM if x.ndim == 1 else pltpu.VMEM)(x.shape, x.dtype) for x in operands
        ]
        partial_sums, tables = pl.pallas_call(
            functools.partial(project_kernel, steps),
            out_shape=(
                jax.ShapeDtypeStruct((rows, (heads + 2) * width), BF16),
                jax.ShapeDtypeStruct((3 * rows, width), F32),
            ),
            in_specs=[anywhere] * 8,
            out_specs=(whole, whole),
            scratch_shapes=buffers + [pltpu.SemaphoreType.DMA((6,))],
            compiler_params=pltpu.CompilerParams(vmem_limit_bytes=4 * 2**20),
        )(*[in_hbm(x) for x in operands], in_hbm(key_cache), in_hbm(value_cache))
    def note(x):
        return pl.pallas_call(
            note_kernel, out_shape=jax.ShapeDtypeStruct(x.shape, x.dtype), in_specs=[whole], out_specs=whole,
            cost_estimate=pl.CostEstimate(flops=0, bytes_accessed=16800000, transcendentals=0),
            compiler_params=pltpu.CompilerParams(vmem_limit_bytes=2**20),
        )(x)

    with jax.named_scope("sum_over_width"):
        along_x = exchange_routes(4, devices // 4, False)
        along_z = exchange_routes(4, devices // 4, True)
        sums = [partial_sums] + [lax.ppermute(partial_sums, "seq", route) for route in along_x]
        sums = functools.reduce(jnp.add, [x.astype(F32) for x in sums]).astype(BF16)
        sums = [sums] + [lax.ppermute(sums, "seq", route) for route in along_z]
    with jax.named_scope("attention"):
        message, new_keys, new_values = pl.pallas_call(
            functools.partial(attend_kernel, steps, heads, 2048, devices),
            out_shape=(
                jax.ShapeDtypeStruct((devices, rows, (heads + 1) * width), BF16),
                jax.ShapeDtypeStruct((steps, batch, width), BF16),
                jax.ShapeDtypeStruct((steps, batch, width), BF16),
            ),
            in_specs=[whole] * 7,
            out_specs=(whole, anywhere, anywhere),
            scratch_shapes=[
                pltpu.VMEM((batch, steps * heads, width), F32),
                pltpu.VMEM((batch, steps * heads, key_cache.shape[1]), F32),
                pltpu.VMEM((rows, (heads + 1) * width), F32),
                pltpu.VMEM((1,8,128), BF16),
                pltpu.VMEM((steps, batch, width), BF16),
                pltpu.VMEM((steps, batch, width), BF16),
                pltpu.SemaphoreType.DMA((batch,)),
                pltpu.SemaphoreType.DMA((2,)),
            ],
            compiler_params=pltpu.CompilerParams(vmem_limit_bytes=16 * 2**20),
        )(tables, *sums, in_vmem(key_cache), in_vmem(value_cache))
    with jax.named_scope("combine"):
        messages = gather_all(message, "seq")
        ranks = lax.axis_size("head") // 2
        part = jax.ShapeDtypeStruct((ranks, rows, HALF), BF16)
        mine, other = pl.pallas_call(
            functools.partial(combine_kernel, heads),
            out_shape=(part, part),
            in_specs=[whole, whole],
            out_specs=(whole, whole),
            compiler_params=pltpu.CompilerParams(vmem_limit_bytes=4 * 2**20),
        )(in_vmem(messages), in_vmem(w_out))
    with jax.named_scope("sum_over_heads"):
        other = lax.ppermute(other, "head", [(i, i ^ 1) for i in range(2 * ranks)])
        pair = mine.astype(F32) + other.astype(F32)
        parts = [pair[0]]
        for d, route in zip((2, 1, 3), exchange_routes(ranks, 2, True, (2, 1, 3))):
            parts.append(lax.ppermute(pair[d], "head", route))
        attn_out = functools.reduce(jnp.add, parts).astype(BF16).reshape(steps, batch, HALF)
    return attn_out, new_keys, new_values


def solution(mesh):
    in_specs = (
        P(None, None, "seq"),
        P("seq", "head"),
        P("seq", "head"),
        P("seq", "head"),
        P("head", "seq"),
        P(None, "seq", "head"),
        P(None, "seq", "head"),
        P(),
    )
    out_specs = (P(None, None, ("seq", "head")), P(None, None, "head"), P(None, None, "head"))
    return jax.shard_map(local, mesh=mesh, in_specs=in_specs, out_specs=out_specs, check_vma=False)
```

```python
import functools

import jax
import jax.numpy as jnp
import numpy as np
from jax import lax
from jax.experimental import pallas as pl
from jax.experimental.pallas import tpu as pltpu
from jax.sharding import PartitionSpec as P

HEAD_WIDTH = 128
HALF = HEAD_WIDTH // 2
THETA = 500000.0
FILL = -1e30
F32 = jnp.float32
BF16 = jnp.bfloat16
VMEM = pltpu.MemorySpace.VMEM


def rotary_tables():
    exponent = np.arange(HALF) * 2.0 / HEAD_WIDTH
    inverse = THETA ** (-exponent)
    coarse = np.mod(1024.0 * inverse, 2.0 * np.pi)
    fine = np.concatenate([inverse, inverse])[None]
    coarse = np.concatenate([coarse, coarse])[None]
    sign = np.where(np.arange(HEAD_WIDTH) < HALF, -1.0, 1.0)[None]
    return np.concatenate([fine, coarse, sign]).astype(np.float32)


def note_kernel(x_ref, o_ref):
    o_ref[...] = x_ref[...]


def project_kernel(
    steps, constants_hbm, lengths_hbm, hidden_hbm, wk_hbm, wv_hbm, wq_hbm, _, __, out_ref, tables_ref,
    constants_ref, lengths_ref, hidden_ref, wk_ref, wv_ref, wq_ref, sems,
):
    pairs = [
        (constants_hbm, constants_ref), (lengths_hbm, lengths_ref), (hidden_hbm, hidden_ref),
        (wk_hbm, wk_ref), (wv_hbm, wv_ref), (wq_hbm, wq_ref),
    ]
    copies = [pltpu.make_async_copy(src, dst, sems.at[i]) for i, (src, dst) in enumerate(pairs)]
    for copy in copies:
        copy.start()
    copies[0].wait()
    copies[1].wait()
    batch = lengths_ref.shape[0]
    rows = steps * batch
    width = constants_ref.shape[1]
    sublane = lax.broadcasted_iota(jnp.int32, (rows, width), 0)
    position = jnp.zeros((rows, width), jnp.int32)
    for r in range(rows):
        s, b = divmod(r, batch)
        position = jnp.where(sublane == r, lengths_ref[b] + s, position)
    upper = jnp.right_shift(position, 10).astype(F32)
    lower = jnp.bitwise_and(position, 1023).astype(F32)
    angles = upper * constants_ref[1:2, :] + lower * constants_ref[0:1, :]
    tables_ref[:rows, :] = jnp.cos(angles)
    tables_ref[rows : 2 * rows, :] = jnp.sin(angles) * constants_ref[2:3, :]
    tables_ref[2 * rows :, :] = position.astype(F32)
    copies[2].wait()
    hidden = jnp.concatenate([hidden_ref[s].astype(F32) for s in range(steps)], axis=0).astype(BF16)
    q_width = wq_ref.shape[1]
    kv_width = wk_ref.shape[1]
    copies[3].wait()
    key = jnp.dot(hidden, wk_ref[...], preferred_element_type=F32)
    copies[4].wait()
    value = jnp.dot(hidden, wv_ref[...], preferred_element_type=F32)
    copies[5].wait()
    query = jnp.dot(hidden, wq_ref[...], preferred_element_type=F32)
    for c in range(out_ref.shape[0]):
        out_ref[c, :, :q_width] = query.astype(BF16)
        out_ref[c, :, q_width : q_width + kv_width] = key.astype(BF16)
        out_ref[c, :, q_width + kv_width :] = value.astype(BF16)


def fetch_kernel(first, source_ref, target_ref, sem):
    batch = target_ref.shape[0]
    copies = [
        pltpu.make_async_copy(source_ref.at[first + b], target_ref.at[b], sem.at[b]) for b in range(batch)
    ]
    for copy in copies:
        copy.start()
    for copy in copies:
        copy.wait()


def attend_kernel(
    steps, heads, chunk, copies, tables_ref, sums_ref, *refs
):
    *keys_refs, values_ref, message_ref, new_keys_hbm, new_values_hbm = refs[:-8]
    query_scr, scores_scr, out_scr, value_buf, new_keys_ref, new_values_ref, value_sems, new_sems = refs[-8:]
    batch, context, width = values_ref.shape
    each = batch // len(keys_refs)

    def fetch(b):
        return pltpu.make_async_copy(values_ref.at[b], value_buf.at[b], value_sems.at[b])

    rows = steps * batch
    group = steps * heads
    total = sums_ref[0].astype(F32)
    for d in range(1, sums_ref.shape[0]):
        total = total + sums_ref[d].astype(F32)
    cosine = tables_ref[:rows]
    sine = tables_ref[rows : 2 * rows]

    def rotate(x):
        return x * cosine + pltpu.roll(x, HALF, 1) * sine

    for h in range(heads):
        rotated = rotate(total[:, h * width : (h + 1) * width]) * (width**-0.5)
        for r in range(rows):
            s, b = divmod(r, batch)
            query_scr[b, s * heads + h : s * heads + h + 1, :] = rotated[r : r + 1]
    new_key = rotate(total[:, heads * width : (heads + 1) * width]).astype(BF16).astype(F32)
    new_value = total[:, (heads + 1) * width :]
    for s in range(steps):
        new_keys_ref[s] = new_key[s * batch : (s + 1) * batch].astype(BF16)
        new_values_ref[s] = new_value[s * batch : (s + 1) * batch].astype(BF16)
    new_copies = [
        pltpu.make_async_copy(new_keys_ref, new_keys_hbm, new_sems.at[0]),
        pltpu.make_async_copy(new_values_ref, new_values_hbm, new_sems.at[1]),
    ]
    for copy in new_copies:
        copy.start()

    seq = lax.axis_index("seq")
    first = seq * context
    owner = seq == 0
    sublane = lax.broadcasted_iota(jnp.int32, (group, width), 0)
    lane = lax.broadcasted_iota(jnp.int32, (group, width), 1)
    stat_lane = lane - sublane % heads
    position = lax.broadcasted_iota(jnp.int32, (group, chunk), 1)
    row_step = lax.broadcasted_iota(jnp.int32, (group, 1), 0) // heads

    tops = []
    for b in range(batch):
        query = query_scr[b].astype(BF16)
        keys_ref = keys_refs[b // each]
        limit = tables_ref[2 * rows + b : 2 * rows + b + 1, :1].astype(jnp.int32) - first
        top = jnp.full((group, chunk), FILL, F32)
        for start in range(0, context, chunk):
            scores = lax.dot_general(
                query, keys_ref[b % each, start : start + chunk, :], (((1,), (1,)), ((), ())),
                preferred_element_type=F32,
            )
            scores = jnp.where(position < limit - start, scores, FILL)
            scores_scr[b, :, start : start + chunk] = scores
            top = jnp.maximum(top, scores)
        tops.append(jnp.max(top, axis=1, keepdims=True))
    for b in range(batch):
        limit = tables_ref[2 * rows + b : 2 * rows + b + 1, :1].astype(jnp.int32) - first
        top = tops[b]
        query_wide = query_scr[b].astype(BF16).astype(F32)
        fresh = []
        for t in range(steps):
            row = t * batch + b
            score = jnp.sum(query_wide * new_key[row : row + 1], axis=1, keepdims=True)
            fresh.append(jnp.where(row_step >= t, score, FILL))
        fresh_top = functools.reduce(jnp.maximum, fresh)
        top = jnp.where(owner, jnp.maximum(top, fresh_top), top)
        top = top.astype(BF16).astype(F32)
        weight_sum = jnp.zeros((group, chunk), F32)
        out = jnp.zeros((group, width), F32)
        for start in range(0, context, chunk):
            weights = jnp.where(
                position < limit - start, jnp.exp(scores_scr[b, :, start : start + chunk] - top), 0.0
            ).astype(BF16)
            weight_sum = weight_sum + weights.astype(F32)
            out = out + jnp.dot(
                weights, values_ref[b, start : start + chunk, :], preferred_element_type=F32
            )
        weight_sum = jnp.sum(weight_sum, axis=1, keepdims=True)
        fresh_scale = jnp.where(owner, jnp.exp(fresh_top - jnp.where(owner, top, fresh_top)), 0.0)
        for t in range(steps):
            row = t * batch + b
            weight = jnp.where(row_step >= t, jnp.exp(fresh[t] - fresh_top), 0.0)
            weight = weight.astype(BF16).astype(F32) * fresh_scale
            weight_sum = weight_sum + weight
            out = out + weight * new_value[row : row + 1]
        sum_high = weight_sum.astype(BF16).astype(F32)
        sum_low = weight_sum - sum_high
        stats = jnp.where(
            stat_lane == 0, top,
            jnp.where(stat_lane == heads, sum_high, jnp.where(stat_lane == 2 * heads, sum_low, 0.0)),
        )
        for s in range(steps):
            r = s * batch + b
            out_scr[r : r + 1, heads * width :] = jnp.sum(
                stats[s * heads : (s + 1) * heads], axis=0, keepdims=True
            )
            for h in range(heads):
                out_scr[r : r + 1, h * width : (h + 1) * width] = out[s * heads + h : s * heads + h + 1]
    message = out_scr[...].astype(BF16)
    for c in range(copies):
        message_ref[c] = message
    for copy in new_copies:
        copy.wait()


def combine_kernel(heads, message_ref, w_out_ref, mine_ref, other_ref):
    devices, rows, _ = message_ref.shape
    width = HEAD_WIDTH
    stats = [message_ref[d, :, heads * width :].astype(F32) for d in range(devices)]
    top = functools.reduce(jnp.maximum, stats)
    total = jnp.zeros((rows, width), F32)
    factors = []
    lane = lax.broadcasted_iota(jnp.int32, (rows, width), 1)
    for d in range(devices):
        factor = jnp.exp(jnp.where(lane < heads, stats[d] - top, 0.0))
        sums = pltpu.roll(stats[d], width - heads, 1) + pltpu.roll(stats[d], width - 2 * heads, 1)
        total = total + factor * sums
        factors.append(factor)
    scale = 1.0 / jnp.where(lane < heads, total, 1.0)
    factors = [f * scale for f in factors]
    attended = []
    for h in range(heads):
        mixed = jnp.zeros((rows, width), F32)
        for d in range(devices):
            part = message_ref[d, :, h * width : (h + 1) * width].astype(F32)
            mixed = mixed + factors[d][:, h : h + 1] * part
        attended.append(mixed.astype(BF16))
    attended = jnp.concatenate(attended, axis=1)
    projected = jnp.dot(attended, w_out_ref[...], preferred_element_type=F32)
    head = lax.axis_index("head")
    rank = head // 2
    first_core = head % 2 == 0
    for target in range(mine_ref.shape[0]):
        block = projected[:, target * width : (target + 1) * width]
        swapped = pltpu.roll(block, HALF, 1)
        slot = jnp.bitwise_xor(rank, target)
        mine_ref[slot] = jnp.where(first_core, block, swapped)[:, :HALF].astype(BF16)
        other_ref[slot] = jnp.where(first_core, swapped, block)[:, :HALF].astype(BF16)


def in_vmem(x):
    return pltpu.with_memory_space_constraint(x, VMEM)


def exchange_routes(count, inner, axis_inner, order=(1, 3, 2)):
    routes = []
    for d in order:
        pairs = []
        for i in range(count):
            for j in range(inner):
                pairs.append((i * inner + j, (i ^ d) * inner + j) if axis_inner else (j * count + i, j * count + (i ^ d)))
        routes.append(pairs)
    return routes


def in_hbm(x):
    return pltpu.with_memory_space_constraint(x, pltpu.MemorySpace.HBM)


def gather_all(x, axis):
    return lax.all_to_all(x, axis, 0, 0, tiled=True)


def local(hidden, w_query, key_matrix, value_matrix, w_out, key_cache, value_cache, lengths):
    steps, batch, _ = hidden.shape
    rows = steps * batch
    width = HEAD_WIDTH
    heads = w_query.shape[1] // width
    devices = lax.axis_size("seq")
    whole = pl.BlockSpec(memory_space=VMEM)
    anywhere = pl.BlockSpec(memory_space=pl.ANY)

    with jax.named_scope("projections"):
        operands = (jnp.asarray(rotary_tables()), lengths, hidden, key_matrix, value_matrix, w_query)
        buffers = [
            (pltpu.SMEM if x.ndim == 1 else pltpu.VMEM)(x.shape, x.dtype) for x in operands
        ]
        partial_sums, tables = pl.pallas_call(
            functools.partial(project_kernel, steps),
            out_shape=(
                jax.ShapeDtypeStruct((devices, rows, (heads + 2) * width), BF16),
                jax.ShapeDtypeStruct((3 * rows, width), F32),
            ),
            in_specs=[anywhere] * 8,
            out_specs=(whole, whole),
            scratch_shapes=buffers + [pltpu.SemaphoreType.DMA((6,))],
            compiler_params=pltpu.CompilerParams(vmem_limit_bytes=4 * 2**20),
        )(*[in_hbm(x) for x in operands], in_hbm(key_cache), in_hbm(value_cache))
    def note(x):
        return pl.pallas_call(
            note_kernel, out_shape=jax.ShapeDtypeStruct(x.shape, x.dtype), in_specs=[whole], out_specs=whole,
            cost_estimate=pl.CostEstimate(flops=0, bytes_accessed=16800000, transcendentals=0),
            compiler_params=pltpu.CompilerParams(vmem_limit_bytes=2**20),
        )(x)

    with jax.named_scope("sum_over_width"):
        sums = gather_all(partial_sums, "seq")
    with jax.named_scope("attention"):
        message, new_keys, new_values = pl.pallas_call(
            functools.partial(attend_kernel, steps, heads, 2048, devices),
            out_shape=(
                jax.ShapeDtypeStruct((devices, rows, (heads + 1) * width), BF16),
                jax.ShapeDtypeStruct((steps, batch, width), BF16),
                jax.ShapeDtypeStruct((steps, batch, width), BF16),
            ),
            in_specs=[whole] * 4,
            out_specs=(whole, anywhere, anywhere),
            scratch_shapes=[
                pltpu.VMEM((batch, steps * heads, width), F32),
                pltpu.VMEM((batch, steps * heads, key_cache.shape[1]), F32),
                pltpu.VMEM((rows, (heads + 1) * width), F32),
                pltpu.VMEM((1,8,128), BF16),
                pltpu.VMEM((steps, batch, width), BF16),
                pltpu.VMEM((steps, batch, width), BF16),
                pltpu.SemaphoreType.DMA((batch,)),
                pltpu.SemaphoreType.DMA((2,)),
            ],
            compiler_params=pltpu.CompilerParams(vmem_limit_bytes=16 * 2**20),
        )(tables, sums, in_vmem(key_cache), in_vmem(value_cache))
    with jax.named_scope("combine"):
        messages = gather_all(message, "seq")
        ranks = lax.axis_size("head") // 2
        part = jax.ShapeDtypeStruct((ranks, rows, HALF), BF16)
        mine, other = pl.pallas_call(
            functools.partial(combine_kernel, heads),
            out_shape=(part, part),
            in_specs=[whole, whole],
            out_specs=(whole, whole),
            compiler_params=pltpu.CompilerParams(vmem_limit_bytes=4 * 2**20),
        )(in_vmem(messages), in_vmem(w_out))
    with jax.named_scope("sum_over_heads"):
        other = lax.ppermute(other, "head", [(i, i ^ 1) for i in range(2 * ranks)])
        pair = mine.astype(F32) + other.astype(F32)
        parts = [pair[0]]
        for d, route in zip((2, 1, 3), exchange_routes(ranks, 2, True, (2, 1, 3))):
            parts.append(lax.ppermute(pair[d], "head", route))
        attn_out = functools.reduce(jnp.add, parts).astype(BF16).reshape(steps, batch, HALF)
    return attn_out, new_keys, new_values


def solution(mesh):
    in_specs = (
        P(None, None, "seq"),
        P("seq", "head"),
        P("seq", "head"),
        P("seq", "head"),
        P("head", "seq"),
        P(None, "seq", "head"),
        P(None, "seq", "head"),
        P(),
    )
    out_specs = (P(None, None, ("seq", "head")), P(None, None, "head"), P(None, None, "head"))
    return jax.shard_map(local, mesh=mesh, in_specs=in_specs, out_specs=out_specs, check_vma=False)
```

```python
import functools

import jax
import jax.numpy as jnp
import numpy as np
from jax import lax
from jax.experimental import pallas as pl
from jax.experimental.pallas import tpu as pltpu
from jax.sharding import PartitionSpec as P

HEAD_WIDTH = 128
HALF = HEAD_WIDTH // 2
THETA = 500000.0
FILL = -1e30
F32 = jnp.float32
BF16 = jnp.bfloat16
VMEM = pltpu.MemorySpace.VMEM


def rotary_tables():
    exponent = np.arange(HALF) * 2.0 / HEAD_WIDTH
    inverse = THETA ** (-exponent)
    coarse = np.mod(1024.0 * inverse, 2.0 * np.pi)
    fine = np.concatenate([inverse, inverse])[None]
    coarse = np.concatenate([coarse, coarse])[None]
    sign = np.where(np.arange(HEAD_WIDTH) < HALF, -1.0, 1.0)[None]
    return np.concatenate([fine, coarse, sign]).astype(np.float32)


def announce_kernel(keys_ref, values_ref, tables_ref, out_ref):
    del keys_ref, values_ref
    out_ref[...] = tables_ref[...]


def project_kernel(
    steps, constants_hbm, lengths_hbm, hidden_hbm, wk_hbm, wv_hbm, wq_hbm, out_ref, tables_ref,
    constants_ref, lengths_ref, hidden_ref, wk_ref, wv_ref, wq_ref, sems,
):
    pairs = [
        (constants_hbm, constants_ref), (lengths_hbm, lengths_ref), (hidden_hbm, hidden_ref),
        (wk_hbm, wk_ref), (wv_hbm, wv_ref), (wq_hbm, wq_ref),
    ]
    copies = [pltpu.make_async_copy(src, dst, sems.at[i]) for i, (src, dst) in enumerate(pairs)]
    for copy in copies:
        copy.start()
    copies[0].wait()
    copies[1].wait()
    batch = lengths_ref.shape[0]
    rows = steps * batch
    width = constants_ref.shape[1]
    sublane = lax.broadcasted_iota(jnp.int32, (rows, width), 0)
    position = jnp.zeros((rows, width), jnp.int32)
    for r in range(rows):
        s, b = divmod(r, batch)
        position = jnp.where(sublane == r, lengths_ref[b] + s, position)
    upper = jnp.right_shift(position, 10).astype(F32)
    lower = jnp.bitwise_and(position, 1023).astype(F32)
    angles = upper * constants_ref[1:2, :] + lower * constants_ref[0:1, :]
    tables_ref[:rows, :] = jnp.cos(angles)
    tables_ref[rows : 2 * rows, :] = jnp.sin(angles) * constants_ref[2:3, :]
    tables_ref[2 * rows :, :] = position.astype(F32)
    copies[2].wait()
    hidden = jnp.concatenate([hidden_ref[s].astype(F32) for s in range(steps)], axis=0).astype(BF16)
    q_width = wq_ref.shape[1]
    kv_width = wk_ref.shape[1]
    copies[3].wait()
    key = jnp.dot(hidden, wk_ref[...], preferred_element_type=F32)
    copies[4].wait()
    value = jnp.dot(hidden, wv_ref[...], preferred_element_type=F32)
    copies[5].wait()
    query = jnp.dot(hidden, wq_ref[...], preferred_element_type=F32)
    for c in range(out_ref.shape[0]):
        out_ref[c, :, :q_width] = query.astype(BF16)
        out_ref[c, :, q_width : q_width + kv_width] = key.astype(BF16)
        out_ref[c, :, q_width + kv_width :] = value.astype(BF16)


def split(x, count):
    parts = []
    for _ in range(count):
        parts.append(x.astype(BF16).astype(F32))
        x = x - parts[-1]
    return parts


def attend_kernel(
    steps, heads, chunk, copies, tables_ref, sums_ref, keys_ref, values_ref, message_ref, new_keys_hbm, new_values_hbm,
    query_scr, scores_scr, out_scr, new_keys_ref, new_values_ref, new_sems,
):
    batch, context, width = values_ref.shape
    rows = steps * batch
    group = steps * heads
    total = sums_ref[0].astype(F32)
    for d in range(1, sums_ref.shape[0]):
        total = total + sums_ref[d].astype(F32)
    cosine = tables_ref[:rows]
    sine = tables_ref[rows : 2 * rows]

    def rotate(x):
        return x * cosine + pltpu.roll(x, HALF, 1) * sine

    for h in range(heads):
        rotated = rotate(total[:, h * width : (h + 1) * width]) * (width**-0.5)
        for r in range(rows):
            s, b = divmod(r, batch)
            query_scr[b, s * heads + h : s * heads + h + 1, :] = rotated[r : r + 1]
    new_key = rotate(total[:, heads * width : (heads + 1) * width]).astype(BF16).astype(F32)
    new_value = total[:, (heads + 1) * width :]
    for s in range(steps):
        new_keys_ref[s] = new_key[s * batch : (s + 1) * batch].astype(BF16)
        new_values_ref[s] = new_value[s * batch : (s + 1) * batch].astype(BF16)
    new_copies = [
        pltpu.make_async_copy(new_keys_ref, new_keys_hbm, new_sems.at[0]),
        pltpu.make_async_copy(new_values_ref, new_values_hbm, new_sems.at[1]),
    ]
    for copy in new_copies:
        copy.start()

    seq = lax.axis_index("seq")
    first = seq * context
    owner = seq == 0
    sublane = lax.broadcasted_iota(jnp.int32, (group, width), 0)
    lane = lax.broadcasted_iota(jnp.int32, (group, width), 1)
    stat_lane = lane - sublane % heads
    position = lax.broadcasted_iota(jnp.int32, (group, chunk), 1)
    row_step = lax.broadcasted_iota(jnp.int32, (group, 1), 0) // heads

    tops = []
    for b in range(batch):
        query = query_scr[b].astype(BF16)
        limit = tables_ref[2 * rows + b : 2 * rows + b + 1, :1].astype(jnp.int32) - first
        top = jnp.full((group, chunk), FILL, F32)
        for start in range(0, context, chunk):
            scores = lax.dot_general(
                query, keys_ref[b, start : start + chunk, :], (((1,), (1,)), ((), ())),
                preferred_element_type=F32,
            )
            scores = jnp.where(position < limit - start, scores, FILL)
            scores_scr[b, :, start : start + chunk] = scores
            top = jnp.maximum(top, scores)
        tops.append(jnp.max(top, axis=1, keepdims=True))
    for b in range(batch):
        limit = tables_ref[2 * rows + b : 2 * rows + b + 1, :1].astype(jnp.int32) - first
        top = tops[b]
        query_wide = query_scr[b].astype(BF16).astype(F32)
        fresh = []
        for t in range(steps):
            row = t * batch + b
            score = jnp.sum(query_wide * new_key[row : row + 1], axis=1, keepdims=True)
            fresh.append(jnp.where(row_step >= t, score, FILL))
        fresh_top = functools.reduce(jnp.maximum, fresh)
        top = jnp.where(owner, jnp.maximum(top, fresh_top), top)
        weight_sum = jnp.zeros((group, chunk), F32)
        out = jnp.zeros((group, width), F32)
        for start in range(0, context, chunk):
            weights = jnp.where(
                position < limit - start, jnp.exp(scores_scr[b, :, start : start + chunk] - top), 0.0
            ).astype(BF16)
            weight_sum = weight_sum + weights.astype(F32)
            out = out + jnp.dot(
                weights, values_ref[b, start : start + chunk, :], preferred_element_type=F32
            )
        weight_sum = jnp.sum(weight_sum, axis=1, keepdims=True)
        fresh_scale = jnp.where(owner, jnp.exp(fresh_top - jnp.where(owner, top, fresh_top)), 0.0)
        for t in range(steps):
            row = t * batch + b
            weight = jnp.where(row_step >= t, jnp.exp(fresh[t] - fresh_top), 0.0)
            weight = weight.astype(BF16).astype(F32) * fresh_scale
            weight_sum = weight_sum + weight
            out = out + weight * new_value[row : row + 1]
        parts = split(top, 3) + split(weight_sum, 2)
        stats = jnp.zeros((group, width), F32)
        for i, part in enumerate(parts):
            stats = jnp.where(stat_lane == i * heads, part, stats)
        for s in range(steps):
            r = s * batch + b
            out_scr[r : r + 1, heads * width :] = jnp.sum(
                stats[s * heads : (s + 1) * heads], axis=0, keepdims=True
            )
            for h in range(heads):
                out_scr[r : r + 1, h * width : (h + 1) * width] = out[s * heads + h : s * heads + h + 1]
    message = out_scr[...].astype(BF16)
    for c in range(copies):
        message_ref[c] = message
    for copy in new_copies:
        copy.wait()


def combine_kernel(heads, message_ref, w_out_ref, out_ref):
    devices, rows, _ = message_ref.shape
    width = HEAD_WIDTH
    lane = lax.broadcasted_iota(jnp.int32, (rows, width), 1)
    tops, sums = [], []
    for d in range(devices):
        stats = message_ref[d, :, heads * width :].astype(F32)
        parts = [stats] + [pltpu.roll(stats, width - i * heads, 1) for i in range(1, 5)]
        tops.append(jnp.where(lane < heads, (parts[0] + parts[1]) + parts[2], 0.0))
        sums.append(parts[3] + parts[4])
    top = functools.reduce(jnp.maximum, tops)
    total = jnp.zeros((rows, width), F32)
    factors = []
    for d in range(devices):
        factors.append(jnp.exp(tops[d] - top))
        total = total + factors[d] * sums[d]
    scale = 1.0 / jnp.where(lane < heads, total, 1.0)
    factors = [f * scale for f in factors]
    attended = []
    for h in range(heads):
        mixed = jnp.zeros((rows, width), F32)
        for d in range(devices):
            part = message_ref[d, :, h * width : (h + 1) * width].astype(F32)
            mixed = mixed + factors[d][:, h : h + 1] * part
        attended.append(mixed.astype(BF16))
    attended = jnp.concatenate(attended, axis=1)
    projected = jnp.dot(attended, w_out_ref[...], preferred_element_type=F32)
    head = lax.axis_index("head")
    rank = head // 2
    for target in range(out_ref.shape[0]):
        slot = jnp.bitwise_xor(rank, target)
        out_ref[slot] = projected[:, target * width : (target + 1) * width].astype(BF16)


def finish_kernel(pair_ref, part1_ref, part2_ref, part3_ref, out_ref):
    total = pair_ref[0]
    for part_ref in (part1_ref, part2_ref, part3_ref):
        total = total + part_ref[...]
    first_core = lax.axis_index("head") % 2 == 0
    total = jnp.where(first_core, total, pltpu.roll(total, HALF, 1))[:, :HALF]
    steps, batch, _ = out_ref.shape
    for s in range(steps):
        out_ref[s] = total[s * batch : (s + 1) * batch].astype(BF16)


def in_vmem(x):
    return pltpu.with_memory_space_constraint(x, VMEM)


def in_hbm(x):
    return pltpu.with_memory_space_constraint(x, pltpu.MemorySpace.HBM)


def gather_all(x, axis):
    return lax.all_to_all(x, axis, 0, 0, tiled=True)


def local(hidden, w_query, key_matrix, value_matrix, w_out, key_cache, value_cache, lengths):
    steps, batch, _ = hidden.shape
    rows = steps * batch
    width = HEAD_WIDTH
    heads = w_query.shape[1] // width
    devices = lax.axis_size("seq")
    whole = pl.BlockSpec(memory_space=VMEM)
    anywhere = pl.BlockSpec(memory_space=pl.ANY)

    with jax.named_scope("projections"):
        operands = (jnp.asarray(rotary_tables()), lengths, hidden, key_matrix, value_matrix, w_query)
        buffers = [(pltpu.SMEM if x.ndim == 1 else pltpu.VMEM)(x.shape, x.dtype) for x in operands]
        partial_sums, tables = pl.pallas_call(
            functools.partial(project_kernel, steps),
            out_shape=(
                jax.ShapeDtypeStruct((devices, rows, (heads + 2) * width), BF16),
                jax.ShapeDtypeStruct((3 * rows, width), F32),
            ),
            in_specs=[anywhere] * 6,
            out_specs=(whole, whole),
            scratch_shapes=buffers + [pltpu.SemaphoreType.DMA((6,))],
            compiler_params=pltpu.CompilerParams(vmem_limit_bytes=4 * 2**20),
        )(*[in_hbm(x) for x in operands])

    def announced(x):
        return pl.pallas_call(
            announce_kernel,
            out_shape=jax.ShapeDtypeStruct(x.shape, x.dtype),
            in_specs=[anywhere, anywhere, whole],
            out_specs=whole,
            compiler_params=pltpu.CompilerParams(vmem_limit_bytes=2**20),
        )(in_hbm(key_cache), in_hbm(value_cache), x)

    with jax.named_scope("sum_over_width"):
        tables = announced(announced(announced(tables)))
        partial_sums, tables = lax.optimization_barrier((partial_sums, tables))
        sums = gather_all(partial_sums, "seq")
    with jax.named_scope("attention"):
        message, new_keys, new_values = pl.pallas_call(
            functools.partial(attend_kernel, steps, heads, 2048, devices),
            out_shape=(
                jax.ShapeDtypeStruct((devices, rows, (heads + 1) * width), BF16),
                jax.ShapeDtypeStruct((steps, batch, width), BF16),
                jax.ShapeDtypeStruct((steps, batch, width), BF16),
            ),
            in_specs=[whole] * 4,
            out_specs=(whole, anywhere, anywhere),
            scratch_shapes=[
                pltpu.VMEM((batch, steps * heads, width), F32),
                pltpu.VMEM((batch, steps * heads, key_cache.shape[1]), F32),
                pltpu.VMEM((rows, (heads + 1) * width), F32),
                pltpu.VMEM((steps, batch, width), BF16),
                pltpu.VMEM((steps, batch, width), BF16),
                pltpu.SemaphoreType.DMA((2,)),
            ],
            compiler_params=pltpu.CompilerParams(vmem_limit_bytes=16 * 2**20),
        )(tables, sums, in_vmem(key_cache), in_vmem(value_cache))
    with jax.named_scope("combine"):
        messages = gather_all(message, "seq")
        ranks = lax.axis_size("head") // 2
        projected = pl.pallas_call(
            functools.partial(combine_kernel, heads),
            out_shape=jax.ShapeDtypeStruct((ranks, rows, width), BF16),
            in_specs=[whole, whole],
            out_specs=whole,
            compiler_params=pltpu.CompilerParams(vmem_limit_bytes=4 * 2**20),
        )(in_vmem(messages), in_vmem(w_out))
    with jax.named_scope("sum_over_heads"):
        other = lax.ppermute(projected, "head", [(i, i ^ 1) for i in range(2 * ranks)])
        pair = projected.astype(F32) + other.astype(F32)
        parts = []
        for d, crossed in ((1, 0), (3, 0), (2, 1)):
            route = [(2 * y + c, 2 * (y ^ d) + (c ^ crossed)) for y in range(ranks) for c in range(2)]
            parts.append(lax.ppermute(pair[d], "head", route))
        attn_out = pl.pallas_call(
            finish_kernel,
            out_shape=jax.ShapeDtypeStruct((steps, batch, HALF), BF16),
            in_specs=[whole] * 4,
            out_specs=whole,
            compiler_params=pltpu.CompilerParams(vmem_limit_bytes=2**20),
        )(pair, *parts)
    return attn_out, new_keys, new_values


def solution(mesh):
    in_specs = (
        P(None, None, "seq"),
        P("seq", "head"),
        P("seq", "head"),
        P("seq", "head"),
        P("head", "seq"),
        P(None, "seq", "head"),
        P(None, "seq", "head"),
        P(),
    )
    out_specs = (P(None, None, ("seq", "head")), P(None, None, "head"), P(None, None, "head"))
    return jax.shard_map(local, mesh=mesh, in_specs=in_specs, out_specs=out_specs, check_vma=False)
```

```python
import functools

import jax
import jax.numpy as jnp
import numpy as np
from jax import lax
from jax.experimental import pallas as pl
from jax.experimental.pallas import tpu as pltpu
from jax.sharding import PartitionSpec as P

HEAD_WIDTH = 128
HALF = HEAD_WIDTH // 2
THETA = 500000.0
FILL = -1e30
F32 = jnp.float32
BF16 = jnp.bfloat16
VMEM = pltpu.MemorySpace.VMEM


def rotary_tables():
    exponent = np.arange(HALF) * 2.0 / HEAD_WIDTH
    inverse = THETA ** (-exponent)
    coarse = np.mod(1024.0 * inverse, 2.0 * np.pi)
    fine = np.concatenate([inverse, inverse])[None]
    coarse = np.concatenate([coarse, coarse])[None]
    sign = np.where(np.arange(HEAD_WIDTH) < HALF, -1.0, 1.0)[None]
    return np.concatenate([fine, coarse, sign]).astype(np.float32)


def announce_kernel(keys_ref, values_ref, tables_ref, out_ref):
    del keys_ref, values_ref
    out_ref[...] = tables_ref[...]


def project_kernel(
    steps, constants_hbm, lengths_hbm, hidden_hbm, wk_hbm, wv_hbm, wq_hbm, out_ref, tables_ref,
    constants_ref, lengths_ref, hidden_ref, wk_ref, wv_ref, wq_ref, sems,
):
    pairs = [
        (constants_hbm, constants_ref), (lengths_hbm, lengths_ref), (hidden_hbm, hidden_ref),
        (wk_hbm, wk_ref), (wv_hbm, wv_ref), (wq_hbm, wq_ref),
    ]
    copies = [pltpu.make_async_copy(src, dst, sems.at[i]) for i, (src, dst) in enumerate(pairs)]
    for copy in copies:
        copy.start()
    copies[0].wait()
    copies[1].wait()
    batch = lengths_ref.shape[0]
    rows = steps * batch
    width = constants_ref.shape[1]
    sublane = lax.broadcasted_iota(jnp.int32, (rows, width), 0)
    position = jnp.zeros((rows, width), jnp.int32)
    for r in range(rows):
        s, b = divmod(r, batch)
        position = jnp.where(sublane == r, lengths_ref[b] + s, position)
    upper = jnp.right_shift(position, 10).astype(F32)
    lower = jnp.bitwise_and(position, 1023).astype(F32)
    angles = upper * constants_ref[1:2, :] + lower * constants_ref[0:1, :]
    tables_ref[:rows, :] = jnp.cos(angles)
    tables_ref[rows : 2 * rows, :] = jnp.sin(angles) * constants_ref[2:3, :]
    tables_ref[2 * rows :, :] = position.astype(F32)
    copies[2].wait()
    hidden = jnp.concatenate([hidden_ref[s].astype(F32) for s in range(steps)], axis=0).astype(BF16)
    q_width = wq_ref.shape[1]
    kv_width = wk_ref.shape[1]
    copies[3].wait()
    key = jnp.dot(hidden, wk_ref[...], preferred_element_type=F32)
    copies[4].wait()
    value = jnp.dot(hidden, wv_ref[...], preferred_element_type=F32)
    copies[5].wait()
    query = jnp.dot(hidden, wq_ref[...], preferred_element_type=F32)
    for c in range(out_ref.shape[0]):
        out_ref[c, :, :q_width] = query.astype(BF16)
        out_ref[c, :, q_width : q_width + kv_width] = key.astype(BF16)
        out_ref[c, :, q_width + kv_width :] = value.astype(BF16)


def split(x, count):
    parts = []
    for _ in range(count):
        parts.append(x.astype(BF16).astype(F32))
        x = x - parts[-1]
    return parts


def attend_kernel(
    steps, heads, chunk, copies, tables_ref, sums_ref, keys_ref, values_ref, message_ref, new_keys_hbm, new_values_hbm,
    query_scr, scores_scr, out_scr, new_keys_ref, new_values_ref, new_sems,
):
    batch, context, width = values_ref.shape
    rows = steps * batch
    group = steps * heads
    total = sums_ref[0].astype(F32)
    for d in range(1, sums_ref.shape[0]):
        total = total + sums_ref[d].astype(F32)
    cosine = tables_ref[:rows]
    sine = tables_ref[rows : 2 * rows]

    def rotate(x):
        return x * cosine + pltpu.roll(x, HALF, 1) * sine

    for h in range(heads):
        rotated = rotate(total[:, h * width : (h + 1) * width]) * (width**-0.5)
        for r in range(rows):
            s, b = divmod(r, batch)
            query_scr[b, s * heads + h : s * heads + h + 1, :] = rotated[r : r + 1]
    new_key = rotate(total[:, heads * width : (heads + 1) * width]).astype(BF16).astype(F32)
    new_value = total[:, (heads + 1) * width :]
    for s in range(steps):
        new_keys_ref[s] = new_key[s * batch : (s + 1) * batch].astype(BF16)
        new_values_ref[s] = new_value[s * batch : (s + 1) * batch].astype(BF16)
    new_copies = [
        pltpu.make_async_copy(new_keys_ref, new_keys_hbm, new_sems.at[0]),
        pltpu.make_async_copy(new_values_ref, new_values_hbm, new_sems.at[1]),
    ]
    for copy in new_copies:
        copy.start()

    seq = lax.axis_index("seq")
    first = seq * context
    owner = seq == 0
    sublane = lax.broadcasted_iota(jnp.int32, (group, width), 0)
    lane = lax.broadcasted_iota(jnp.int32, (group, width), 1)
    stat_lane = lane - sublane % heads
    position = lax.broadcasted_iota(jnp.int32, (group, chunk), 1)
    row_step = lax.broadcasted_iota(jnp.int32, (group, 1), 0) // heads

    tops = []
    for b in range(batch):
        query = query_scr[b].astype(BF16)
        limit = tables_ref[2 * rows + b : 2 * rows + b + 1, :1].astype(jnp.int32) - first
        top = jnp.full((group, chunk), FILL, F32)
        for start in range(0, context, chunk):
            scores = lax.dot_general(
                query, keys_ref[b, start : start + chunk, :], (((1,), (1,)), ((), ())),
                preferred_element_type=F32,
            )
            scores = jnp.where(position < limit - start, scores, FILL)
            scores_scr[b, :, start : start + chunk] = scores
            top = jnp.maximum(top, scores)
        tops.append(jnp.max(top, axis=1, keepdims=True))
    for b in range(batch):
        limit = tables_ref[2 * rows + b : 2 * rows + b + 1, :1].astype(jnp.int32) - first
        top = tops[b]
        query_wide = query_scr[b].astype(BF16).astype(F32)
        fresh = []
        for t in range(steps):
            row = t * batch + b
            score = jnp.sum(query_wide * new_key[row : row + 1], axis=1, keepdims=True)
            fresh.append(jnp.where(row_step >= t, score, FILL))
        fresh_top = functools.reduce(jnp.maximum, fresh)
        top = jnp.where(owner, jnp.maximum(top, fresh_top), top)
        weight_sum = jnp.zeros((group, chunk), F32)
        out = jnp.zeros((group, width), F32)
        for start in range(0, context, chunk):
            weights = jnp.where(
                position < limit - start, jnp.exp(scores_scr[b, :, start : start + chunk] - top), 0.0
            ).astype(BF16)
            weight_sum = weight_sum + weights.astype(F32)
            out = out + jnp.dot(
                weights, values_ref[b, start : start + chunk, :], preferred_element_type=F32
            )
        weight_sum = jnp.sum(weight_sum, axis=1, keepdims=True)
        fresh_scale = jnp.where(owner, jnp.exp(fresh_top - jnp.where(owner, top, fresh_top)), 0.0)
        for t in range(steps):
            row = t * batch + b
            weight = jnp.where(row_step >= t, jnp.exp(fresh[t] - fresh_top), 0.0)
            weight = weight.astype(BF16).astype(F32) * fresh_scale
            weight_sum = weight_sum + weight
            out = out + weight * new_value[row : row + 1]
        parts = split(top, 3) + split(weight_sum, 2)
        stats = jnp.zeros((group, width), F32)
        for i, part in enumerate(parts):
            stats = jnp.where(stat_lane == i * heads, part, stats)
        for s in range(steps):
            r = s * batch + b
            out_scr[r : r + 1, heads * width :] = jnp.sum(
                stats[s * heads : (s + 1) * heads], axis=0, keepdims=True
            )
            for h in range(heads):
                out_scr[r : r + 1, h * width : (h + 1) * width] = out[s * heads + h : s * heads + h + 1]
    message = out_scr[...].astype(BF16)
    for c in range(copies):
        message_ref[c] = message
    for copy in new_copies:
        copy.wait()


def combine_kernel(heads, message_ref, w_out_ref, out_ref):
    devices, rows, _ = message_ref.shape
    width = HEAD_WIDTH
    lane = lax.broadcasted_iota(jnp.int32, (rows, width), 1)
    tops, sums = [], []
    for d in range(devices):
        stats = message_ref[d, :, heads * width :].astype(F32)
        parts = [stats] + [pltpu.roll(stats, width - i * heads, 1) for i in range(1, 5)]
        tops.append(jnp.where(lane < heads, (parts[0] + parts[1]) + parts[2], 0.0))
        sums.append(parts[3] + parts[4])
    top = functools.reduce(jnp.maximum, tops)
    total = jnp.zeros((rows, width), F32)
    factors = []
    for d in range(devices):
        factors.append(jnp.exp(tops[d] - top))
        total = total + factors[d] * sums[d]
    scale = 1.0 / jnp.where(lane < heads, total, 1.0)
    factors = [f * scale for f in factors]
    projected = jnp.zeros((rows, w_out_ref.shape[1]), F32)
    for first in range(0, heads, 2):
        attended = []
        for h in range(first, first + 2):
            mixed = jnp.zeros((rows, width), F32)
            for d in range(devices):
                part = message_ref[d, :, h * width : (h + 1) * width].astype(F32)
                mixed = mixed + factors[d][:, h : h + 1] * part
            attended.append(mixed.astype(BF16))
        rows_of_w = w_out_ref[first * width : (first + 2) * width, :]
        projected = projected + jnp.dot(
            jnp.concatenate(attended, axis=1), rows_of_w, preferred_element_type=F32
        )
    head = lax.axis_index("head")
    rank = head // 2
    for target in range(out_ref.shape[0]):
        slot = jnp.bitwise_xor(rank, target)
        out_ref[slot] = projected[:, target * width : (target + 1) * width].astype(BF16)


def finish_kernel(pair_ref, part1_ref, part2_ref, part3_ref, out_ref):
    total = pair_ref[0]
    for part_ref in (part1_ref, part2_ref, part3_ref):
        total = total + part_ref[...]
    first_core = lax.axis_index("head") % 2 == 0
    total = jnp.where(first_core, total, pltpu.roll(total, HALF, 1))[:, :HALF]
    steps, batch, _ = out_ref.shape
    for s in range(steps):
        out_ref[s] = total[s * batch : (s + 1) * batch].astype(BF16)


def in_vmem(x):
    return pltpu.with_memory_space_constraint(x, VMEM)


def in_hbm(x):
    return pltpu.with_memory_space_constraint(x, pltpu.MemorySpace.HBM)


def gather_all(x, axis):
    return lax.all_to_all(x, axis, 0, 0, tiled=True)


def local(hidden, w_query, key_matrix, value_matrix, w_out, key_cache, value_cache, lengths):
    steps, batch, _ = hidden.shape
    rows = steps * batch
    width = HEAD_WIDTH
    heads = w_query.shape[1] // width
    devices = lax.axis_size("seq")
    whole = pl.BlockSpec(memory_space=VMEM)
    anywhere = pl.BlockSpec(memory_space=pl.ANY)

    with jax.named_scope("projections"):
        operands = (jnp.asarray(rotary_tables()), lengths, hidden, key_matrix, value_matrix, w_query)
        buffers = [(pltpu.SMEM if x.ndim == 1 else pltpu.VMEM)(x.shape, x.dtype) for x in operands]
        partial_sums, tables = pl.pallas_call(
            functools.partial(project_kernel, steps),
            out_shape=(
                jax.ShapeDtypeStruct((devices, rows, (heads + 2) * width), BF16),
                jax.ShapeDtypeStruct((3 * rows, width), F32),
            ),
            in_specs=[anywhere] * 6,
            out_specs=(whole, whole),
            scratch_shapes=buffers + [pltpu.SemaphoreType.DMA((6,))],
            compiler_params=pltpu.CompilerParams(vmem_limit_bytes=4 * 2**20),
        )(*[in_hbm(x) for x in operands])

    def announced(x):
        return pl.pallas_call(
            announce_kernel,
            out_shape=jax.ShapeDtypeStruct(x.shape, x.dtype),
            in_specs=[anywhere, anywhere, whole],
            out_specs=whole,
            compiler_params=pltpu.CompilerParams(vmem_limit_bytes=2**20),
        )(in_hbm(key_cache), in_hbm(value_cache), x)

    with jax.named_scope("sum_over_width"):
        tables = announced(announced(announced(tables)))
        partial_sums, tables = lax.optimization_barrier((partial_sums, tables))
        sums = gather_all(partial_sums, "seq")
    with jax.named_scope("attention"):
        message, new_keys, new_values = pl.pallas_call(
            functools.partial(attend_kernel, steps, heads, 2048, devices),
            out_shape=(
                jax.ShapeDtypeStruct((devices, rows, (heads + 1) * width), BF16),
                jax.ShapeDtypeStruct((steps, batch, width), BF16),
                jax.ShapeDtypeStruct((steps, batch, width), BF16),
            ),
            in_specs=[whole] * 4,
            out_specs=(whole, anywhere, anywhere),
            scratch_shapes=[
                pltpu.VMEM((batch, steps * heads, width), F32),
                pltpu.VMEM((batch, steps * heads, key_cache.shape[1]), F32),
                pltpu.VMEM((rows, (heads + 1) * width), F32),
                pltpu.VMEM((steps, batch, width), BF16),
                pltpu.VMEM((steps, batch, width), BF16),
                pltpu.SemaphoreType.DMA((2,)),
            ],
            compiler_params=pltpu.CompilerParams(vmem_limit_bytes=16 * 2**20),
        )(tables, sums, in_vmem(key_cache), in_vmem(value_cache))
    with jax.named_scope("combine"):
        messages = gather_all(message, "seq")
        ranks = lax.axis_size("head") // 2
        projected = pl.pallas_call(
            functools.partial(combine_kernel, heads),
            out_shape=jax.ShapeDtypeStruct((ranks, rows, width), BF16),
            in_specs=[whole, whole],
            out_specs=whole,
            compiler_params=pltpu.CompilerParams(vmem_limit_bytes=4 * 2**20),
        )(in_vmem(messages), in_vmem(w_out))
    with jax.named_scope("sum_over_heads"):
        other = lax.ppermute(projected, "head", [(i, i ^ 1) for i in range(2 * ranks)])
        pair = projected.astype(F32) + other.astype(F32)
        parts = []
        for d, crossed in ((1, 0), (3, 0), (2, 1)):
            route = [(2 * y + c, 2 * (y ^ d) + (c ^ crossed)) for y in range(ranks) for c in range(2)]
            parts.append(lax.ppermute(pair[d], "head", route))
        attn_out = pl.pallas_call(
            finish_kernel,
            out_shape=jax.ShapeDtypeStruct((steps, batch, HALF), BF16),
            in_specs=[whole] * 4,
            out_specs=whole,
            compiler_params=pltpu.CompilerParams(vmem_limit_bytes=2**20),
        )(pair, *parts)
    return attn_out, new_keys, new_values


def solution(mesh):
    in_specs = (
        P(None, None, "seq"),
        P("seq", "head"),
        P("seq", "head"),
        P("seq", "head"),
        P("head", "seq"),
        P(None, "seq", "head"),
        P(None, "seq", "head"),
        P(),
    )
    out_specs = (P(None, None, ("seq", "head")), P(None, None, "head"), P(None, None, "head"))
    return jax.shard_map(local, mesh=mesh, in_specs=in_specs, out_specs=out_specs, check_vma=False)
```

```python
import functools

import jax
import jax.numpy as jnp
import numpy as np
from jax import lax
from jax.experimental import pallas as pl
from jax.experimental.pallas import tpu as pltpu
from jax.sharding import PartitionSpec as P

HEAD_WIDTH = 128
HALF = HEAD_WIDTH // 2
THETA = 500000.0
FILL = -1e30
F32 = jnp.float32
BF16 = jnp.bfloat16
VMEM = pltpu.MemorySpace.VMEM


def rotary_tables():
    exponent = np.arange(HALF) * 2.0 / HEAD_WIDTH
    inverse = THETA ** (-exponent)
    coarse = np.mod(1024.0 * inverse, 2.0 * np.pi)
    fine = np.concatenate([inverse, inverse])[None]
    coarse = np.concatenate([coarse, coarse])[None]
    sign = np.where(np.arange(HEAD_WIDTH) < HALF, -1.0, 1.0)[None]
    return np.concatenate([fine, coarse, sign]).astype(np.float32)


def announce_kernel(keys_ref, values_ref, tables_ref, out_ref):
    del keys_ref, values_ref
    out_ref[...] = tables_ref[...]


def project_kernel(
    steps, constants_hbm, lengths_hbm, hidden_hbm, wk_hbm, wv_hbm, wq_hbm, out_ref, tables_ref,
    constants_ref, lengths_ref, hidden_ref, wk_ref, wv_ref, wq_ref, sems,
):
    pairs = [
        (constants_hbm, constants_ref), (lengths_hbm, lengths_ref), (hidden_hbm, hidden_ref),
        (wk_hbm, wk_ref), (wv_hbm, wv_ref), (wq_hbm, wq_ref),
    ]
    copies = [pltpu.make_async_copy(src, dst, sems.at[i]) for i, (src, dst) in enumerate(pairs)]
    for copy in copies:
        copy.start()
    copies[0].wait()
    copies[1].wait()
    batch = lengths_ref.shape[0]
    rows = steps * batch
    width = constants_ref.shape[1]
    sublane = lax.broadcasted_iota(jnp.int32, (rows, width), 0)
    position = jnp.zeros((rows, width), jnp.int32)
    for r in range(rows):
        s, b = divmod(r, batch)
        position = jnp.where(sublane == r, lengths_ref[b] + s, position)
    upper = jnp.right_shift(position, 10).astype(F32)
    lower = jnp.bitwise_and(position, 1023).astype(F32)
    angles = upper * constants_ref[1:2, :] + lower * constants_ref[0:1, :]
    tables_ref[:rows, :] = jnp.cos(angles)
    tables_ref[rows : 2 * rows, :] = jnp.sin(angles) * constants_ref[2:3, :]
    tables_ref[2 * rows :, :] = position.astype(F32)
    copies[2].wait()
    hidden = jnp.concatenate([hidden_ref[s].astype(F32) for s in range(steps)], axis=0).astype(BF16)
    q_width = wq_ref.shape[1]
    kv_width = wk_ref.shape[1]
    copies[3].wait()
    key = jnp.dot(hidden, wk_ref[...], preferred_element_type=F32)
    copies[4].wait()
    value = jnp.dot(hidden, wv_ref[...], preferred_element_type=F32)
    copies[5].wait()
    query = jnp.dot(hidden, wq_ref[...], preferred_element_type=F32)
    for c in range(out_ref.shape[0]):
        out_ref[c, :, :q_width] = query.astype(BF16)
        out_ref[c, :, q_width : q_width + kv_width] = key.astype(BF16)
        out_ref[c, :, q_width + kv_width :] = value.astype(BF16)


def split(x, count):
    parts = []
    for _ in range(count):
        parts.append(x.astype(BF16).astype(F32))
        x = x - parts[-1]
    return parts


def attend_kernel(
    steps, heads, chunk, copies, tables_ref, sums_ref, keys_ref, values_ref, message_ref, new_keys_hbm, new_values_hbm,
    query_scr, scores_scr, out_scr, new_keys_ref, new_values_ref, new_sems,
):
    batch, context, width = values_ref.shape
    rows = steps * batch
    group = steps * heads
    total = sums_ref[0].astype(F32)
    for d in range(1, sums_ref.shape[0]):
        total = total + sums_ref[d].astype(F32)
    cosine = tables_ref[:rows]
    sine = tables_ref[rows : 2 * rows]

    def rotate(x):
        return x * cosine + pltpu.roll(x, HALF, 1) * sine

    for h in range(heads):
        rotated = rotate(total[:, h * width : (h + 1) * width]) * (width**-0.5)
        for r in range(rows):
            s, b = divmod(r, batch)
            query_scr[b, s * heads + h : s * heads + h + 1, :] = rotated[r : r + 1]
    new_key = rotate(total[:, heads * width : (heads + 1) * width]).astype(BF16).astype(F32)
    new_value = total[:, (heads + 1) * width :]
    for s in range(steps):
        new_keys_ref[s] = new_key[s * batch : (s + 1) * batch].astype(BF16)
        new_values_ref[s] = new_value[s * batch : (s + 1) * batch].astype(BF16)
    new_copies = [
        pltpu.make_async_copy(new_keys_ref, new_keys_hbm, new_sems.at[0]),
        pltpu.make_async_copy(new_values_ref, new_values_hbm, new_sems.at[1]),
    ]
    for copy in new_copies:
        copy.start()

    seq = lax.axis_index("seq")
    first = seq * context
    owner = seq == 0
    sublane = lax.broadcasted_iota(jnp.int32, (group, width), 0)
    lane = lax.broadcasted_iota(jnp.int32, (group, width), 1)
    stat_lane = lane - sublane % heads
    position = lax.broadcasted_iota(jnp.int32, (group, chunk), 1)
    row_step = lax.broadcasted_iota(jnp.int32, (group, 1), 0) // heads

    tops = []
    for b in range(batch):
        query = query_scr[b].astype(BF16)
        limit = tables_ref[2 * rows + b : 2 * rows + b + 1, :1].astype(jnp.int32) - first
        top = jnp.full((group, chunk), FILL, F32)
        for start in range(0, context, chunk):
            scores = lax.dot_general(
                query, keys_ref[b, start : start + chunk, :], (((1,), (1,)), ((), ())),
                preferred_element_type=F32,
            )
            scores = jnp.where(position < limit - start, scores, FILL)
            scores_scr[b, :, start : start + chunk] = scores
            top = jnp.maximum(top, scores)
        tops.append(jnp.max(top, axis=1, keepdims=True))
    for b in range(batch):
        limit = tables_ref[2 * rows + b : 2 * rows + b + 1, :1].astype(jnp.int32) - first
        top = tops[b]
        query_wide = query_scr[b].astype(BF16).astype(F32)
        fresh = []
        for t in range(steps):
            row = t * batch + b
            score = jnp.sum(query_wide * new_key[row : row + 1], axis=1, keepdims=True)
            fresh.append(jnp.where(row_step >= t, score, FILL))
        fresh_top = functools.reduce(jnp.maximum, fresh)
        top = jnp.where(owner, jnp.maximum(top, fresh_top), top)
        weight_sum = jnp.zeros((group, chunk), F32)
        out = jnp.zeros((group, width), F32)
        for start in range(0, context, chunk):
            weights = jnp.where(
                position < limit - start, jnp.exp(scores_scr[b, :, start : start + chunk] - top), 0.0
            ).astype(BF16)
            weight_sum = weight_sum + weights.astype(F32)
            out = out + jnp.dot(
                weights, values_ref[b, start : start + chunk, :], preferred_element_type=F32
            )
        weight_sum = jnp.sum(weight_sum, axis=1, keepdims=True)
        fresh_scale = jnp.where(owner, jnp.exp(fresh_top - jnp.where(owner, top, fresh_top)), 0.0)
        for t in range(steps):
            row = t * batch + b
            weight = jnp.where(row_step >= t, jnp.exp(fresh[t] - fresh_top), 0.0)
            weight = weight.astype(BF16).astype(F32) * fresh_scale
            weight_sum = weight_sum + weight
            out = out + weight * new_value[row : row + 1]
        parts = split(top, 3) + split(weight_sum, 2)
        stats = jnp.zeros((group, width), F32)
        for i, part in enumerate(parts):
            stats = jnp.where(stat_lane == i * heads, part, stats)
        for s in range(steps):
            r = s * batch + b
            out_scr[r : r + 1, heads * width :] = jnp.sum(
                stats[s * heads : (s + 1) * heads], axis=0, keepdims=True
            )
            for h in range(heads):
                out_scr[r : r + 1, h * width : (h + 1) * width] = out[s * heads + h : s * heads + h + 1]
    message = out_scr[...].astype(BF16)
    for c in range(copies):
        message_ref[c] = message
    for copy in new_copies:
        copy.wait()


def combine_kernel(heads, message_ref, w_out_ref, out_ref):
    devices, rows, _ = message_ref.shape
    width = HEAD_WIDTH
    lane = lax.broadcasted_iota(jnp.int32, (rows, width), 1)
    tops, sums = [], []
    for d in range(devices):
        stats = message_ref[d, :, heads * width :].astype(F32)
        parts = [stats] + [pltpu.roll(stats, width - i * heads, 1) for i in range(1, 5)]
        tops.append(jnp.where(lane < heads, (parts[0] + parts[1]) + parts[2], 0.0))
        sums.append(parts[3] + parts[4])
    top = functools.reduce(jnp.maximum, tops)
    total = jnp.zeros((rows, width), F32)
    factors = []
    for d in range(devices):
        factors.append(jnp.exp(tops[d] - top))
        total = total + factors[d] * sums[d]
    scale = 1.0 / jnp.where(lane < heads, total, 1.0)
    factors = [f * scale for f in factors]
    attended = []
    for h in range(heads):
        mixed = jnp.zeros((rows, width), F32)
        for d in range(devices):
            part = message_ref[d, :, h * width : (h + 1) * width].astype(F32)
            mixed = mixed + factors[d][:, h : h + 1] * part
        attended.append(mixed.astype(BF16))
    attended = jnp.concatenate(attended, axis=1)
    projected = jnp.dot(attended, w_out_ref[...], preferred_element_type=F32)
    head = lax.axis_index("head")
    rank = head // 2
    for target in range(out_ref.shape[0]):
        slot = jnp.bitwise_xor(rank, target)
        out_ref[slot] = projected[:, target * width : (target + 1) * width].astype(BF16)


def finish_kernel(pair_ref, part1_ref, part2_ref, part3_ref, out_ref):
    total = pair_ref[0]
    for part_ref in (part1_ref, part2_ref, part3_ref):
        total = total + part_ref[...]
    first_core = lax.axis_index("head") % 2 == 0
    total = jnp.where(first_core, total, pltpu.roll(total, HALF, 1))[:, :HALF]
    steps, batch, _ = out_ref.shape
    for s in range(steps):
        out_ref[s] = total[s * batch : (s + 1) * batch].astype(BF16)


def in_vmem(x):
    return pltpu.with_memory_space_constraint(x, VMEM)


def in_hbm(x):
    return pltpu.with_memory_space_constraint(x, pltpu.MemorySpace.HBM)


def gather_all(x, axis):
    return lax.all_to_all(x, axis, 0, 0, tiled=True)


def local(hidden, w_query, key_matrix, value_matrix, w_out, key_cache, value_cache, lengths):
    steps, batch, _ = hidden.shape
    rows = steps * batch
    width = HEAD_WIDTH
    heads = w_query.shape[1] // width
    devices = lax.axis_size("seq")
    whole = pl.BlockSpec(memory_space=VMEM)
    anywhere = pl.BlockSpec(memory_space=pl.ANY)

    with jax.named_scope("projections"):
        operands = (jnp.asarray(rotary_tables()), lengths, hidden, key_matrix, value_matrix, w_query)
        buffers = [(pltpu.SMEM if x.ndim == 1 else pltpu.VMEM)(x.shape, x.dtype) for x in operands]
        partial_sums, tables = pl.pallas_call(
            functools.partial(project_kernel, steps),
            out_shape=(
                jax.ShapeDtypeStruct((devices, rows, (heads + 2) * width), BF16),
                jax.ShapeDtypeStruct((3 * rows, width), F32),
            ),
            in_specs=[anywhere] * 6,
            out_specs=(whole, whole),
            scratch_shapes=buffers + [pltpu.SemaphoreType.DMA((6,))],
            compiler_params=pltpu.CompilerParams(vmem_limit_bytes=4 * 2**20),
        )(*[in_hbm(x) for x in operands])

    def announced(x):
        return pl.pallas_call(
            announce_kernel,
            out_shape=jax.ShapeDtypeStruct(x.shape, x.dtype),
            in_specs=[anywhere, anywhere, whole],
            out_specs=whole,
            compiler_params=pltpu.CompilerParams(vmem_limit_bytes=2**20),
        )(in_hbm(key_cache), in_hbm(value_cache), x)

    with jax.named_scope("sum_over_width"):
        tables = announced(announced(announced(tables)))
        partial_sums, tables = lax.optimization_barrier((partial_sums, tables))
        sums = gather_all(partial_sums, "seq")
    with jax.named_scope("attention"):
        message, new_keys, new_values = pl.pallas_call(
            functools.partial(attend_kernel, steps, heads, key_cache.shape[1], devices),
            out_shape=(
                jax.ShapeDtypeStruct((devices, rows, (heads + 1) * width), BF16),
                jax.ShapeDtypeStruct((steps, batch, width), BF16),
                jax.ShapeDtypeStruct((steps, batch, width), BF16),
            ),
            in_specs=[whole] * 4,
            out_specs=(whole, anywhere, anywhere),
            scratch_shapes=[
                pltpu.VMEM((batch, steps * heads, width), F32),
                pltpu.VMEM((batch, steps * heads, key_cache.shape[1]), F32),
                pltpu.VMEM((rows, (heads + 1) * width), F32),
                pltpu.VMEM((steps, batch, width), BF16),
                pltpu.VMEM((steps, batch, width), BF16),
                pltpu.SemaphoreType.DMA((2,)),
            ],
            compiler_params=pltpu.CompilerParams(vmem_limit_bytes=16 * 2**20),
        )(tables, sums, in_vmem(key_cache), in_vmem(value_cache))
    with jax.named_scope("combine"):
        messages = gather_all(message, "seq")
        ranks = lax.axis_size("head") // 2
        projected = pl.pallas_call(
            functools.partial(combine_kernel, heads),
            out_shape=jax.ShapeDtypeStruct((ranks, rows, width), BF16),
            in_specs=[whole, whole],
            out_specs=whole,
            compiler_params=pltpu.CompilerParams(vmem_limit_bytes=4 * 2**20),
        )(in_vmem(messages), in_vmem(w_out))
    with jax.named_scope("sum_over_heads"):
        other = lax.ppermute(projected, "head", [(i, i ^ 1) for i in range(2 * ranks)])
        pair = projected.astype(F32) + other.astype(F32)
        parts = []
        for d, crossed in ((1, 0), (3, 0), (2, 1)):
            route = [(2 * y + c, 2 * (y ^ d) + (c ^ crossed)) for y in range(ranks) for c in range(2)]
            parts.append(lax.ppermute(pair[d], "head", route))
        attn_out = pl.pallas_call(
            finish_kernel,
            out_shape=jax.ShapeDtypeStruct((steps, batch, HALF), BF16),
            in_specs=[whole] * 4,
            out_specs=whole,
            compiler_params=pltpu.CompilerParams(vmem_limit_bytes=2**20),
        )(pair, *parts)
    return attn_out, new_keys, new_values


def solution(mesh):
    in_specs = (
        P(None, None, "seq"),
        P("seq", "head"),
        P("seq", "head"),
        P("seq", "head"),
        P("head", "seq"),
        P(None, "seq", "head"),
        P(None, "seq", "head"),
        P(),
    )
    out_specs = (P(None, None, ("seq", "head")), P(None, None, "head"), P(None, None, "head"))
    return jax.shard_map(local, mesh=mesh, in_specs=in_specs, out_specs=out_specs, check_vma=False)
```
